512 devices in a mesh: replica: 16 (over y_lo, x), fsdp: 32 (over z, y_hi, core).
Axes of the slice: x: 4, y: 8 (y_hi: 2, y_lo: 4; y = y_hi * 4 + y_lo), z: 8, core: 2. Of those that a mesh axis runs over, the one named last changes fastest.
Arguments:
- base_weights: float32 [8192, 1024], P('fsdp'), may hold values from -5 to 5, as said below
- inner_weights: bfloat16 [16, 8192, 1024], P('replica', 'fsdp'), may hold values from -12 to 12, as said below
- momentum: float32 [8192, 1024], P(('fsdp', 'replica')), may hold values from -1 to 1
Outputs:
- new_base: float32 [8192, 1024], P('fsdp')
- new_momentum: float32 [8192, 1024], P(('fsdp', 'replica'))
- new_inner: bfloat16 [16, 8192, 1024], P('replica', 'fsdp')
The draws below stay inside these ranges and needn't reach their ends.
Inputs may be any that keep to these rules, and one draw needn't show every extreme that they name: `base_weights`: the shared outer weights, multiples of 2 ** -16. `inner_weights`: each replica's weights after its inner steps, multiples of 2 ** -16.
All inputs are finite; a program needn't handle non-finite values.
Results may differ from the reference program's by a relative error of at most 0.0015.
Values may be sent and summed in bfloat16 or wider, within the bound.
No kernel may reach another device: no remote copies, remote signals or barrier semaphores. Data moves between devices by JAX's collectives and lax.ppermute only.
A program may use at most 64 MiB of HBM per device.

```python
import jax
import jax.numpy as jnp
from jax import lax

D = 8192
KVW = 1024
BLOCK = 128
REPLICAS = 16


grid_step = 65536.0


def draw_common(key):
    folded = jax.random.fold_in(key, 11)
    base_key = jax.random.fold_in(folded, 0)
    column_key = jax.random.fold_in(folded, 1)
    own_key = jax.random.fold_in(folded, 2)
    row_key = jax.random.fold_in(folded, 4)
    base_values = jnp.clip(jax.random.normal(base_key, (D, KVW), jnp.float32), -5.0, 5.0)
    base_values = jnp.floor(base_values * grid_step + 0.5) / grid_step
    columns = jnp.exp(jax.random.uniform(column_key, (KVW,), jnp.float32, 0.0, jnp.log(10.0)))
    row_scale = 0.1 * jnp.exp(jax.random.uniform(row_key, (D,), jnp.float32, -jnp.log(1000.0), 0.0))
    copies = jnp.exp(jnp.log(3.0) * jnp.arange(REPLICAS, dtype=jnp.float32) / (REPLICAS - 1))
    own_noise = jax.random.uniform(own_key, (REPLICAS, D, KVW), jnp.float32, -1.0, 1.0)
    perturb = own_noise
    deltas = perturb * row_scale[None, :, None] * columns[None, None, :] * copies[:, None, None]
    inner_values = base_values[None] - deltas
    inner_values = jnp.floor(inner_values * grid_step + 0.5) / grid_step
    return (base_values, inner_values)


def draw_base_weights(key, part):
    base_values, inner_values = draw_common(key)
    return base_values.astype(jnp.float32)


def draw_inner_weights(key, part):
    base_values, inner_values = draw_common(key)
    return inner_values.astype(jnp.bfloat16)


def levels(key, dims, pieces, low, top_value):
    def one(axis_at, parts):
        draws = jax.random.uniform(jax.random.fold_in(jax.random.fold_in(key, 6), axis_at), (parts,), jnp.float32, low / len(pieces), top_value / len(pieces))
        return jnp.repeat(jnp.exp(draws), dims[axis_at] // parts).reshape((-1,) + (1,) * (len(dims) - axis_at - 1))

    gain = one(*pieces[0])
    for cut in pieces[1:]:
        gain = gain * one(*cut)
    return gain


def scatter_about(key, dims, spread, most, pieces=(), held_as=jnp.bfloat16):
    factor_of = levels(key, dims, pieces, -0.22, 0.18) if pieces else 1.0
    array = jax.random.normal(key, dims, jnp.float32) * spread * factor_of
    return jnp.minimum(jnp.maximum(array, -most), most).astype(held_as)


def setup_inputs(seed: int = 0) -> dict:
    key_of = jax.random.split(jax.random.key(seed), 4)
    return {
        "base_weights": draw_base_weights(jax.random.fold_in(key_of[3], 71), 0),
        "inner_weights": draw_inner_weights(jax.random.fold_in(key_of[3], 71), 0),
        "momentum": scatter_about(key_of[2], (D, KVW), 0.2, 1.0, ((0, 512),), jnp.float32),
    }


code_limit = 448.0
outer_rate = 0.7
outer_momentum = 0.9
blend_share = 0.5
clip_rms = 0.02
epsilon = 1e-06
smallest_normal = 0.015625

def power_two(exponent):
    unit_ones = jnp.ones_like(exponent)
    upward = jnp.left_shift(unit_ones, jnp.maximum(exponent, 0)).astype(jnp.float32)
    downward = jnp.left_shift(unit_ones, jnp.maximum(-exponent, 0)).astype(jnp.float32)
    return upward / downward

def exponent_above(target):
    estimate = jnp.ceil(jnp.log2(target)).astype(jnp.int32)
    estimate = jnp.where(target <= power_two(estimate - 1), estimate - 1, estimate)
    return jnp.where(target > power_two(estimate), estimate + 1, estimate)

def exponent_below(target):
    estimate = jnp.floor(jnp.log2(target)).astype(jnp.int32)
    estimate = jnp.where(target >= power_two(estimate + 1), estimate + 1, estimate)
    return jnp.where(target < power_two(estimate), estimate - 1, estimate)

def encode(deltas):
    shaped = deltas.reshape(deltas.shape[0], deltas.shape[1] // BLOCK, BLOCK)
    block_peaks = lax.optimization_barrier(jnp.max(jnp.abs(shaped), axis=2))
    scales = power_two(exponent_above((block_peaks + epsilon) / code_limit))
    code_units = shaped / scales[:, :, None]
    magnitude = jnp.abs(code_units)
    quantum = power_two(exponent_below(jnp.maximum(magnitude, smallest_normal)) - 3)
    steps_count = jnp.floor(magnitude / quantum + 0.5)
    code_values = (jnp.where(code_units < 0, -steps_count, steps_count) * quantum).astype(jnp.bfloat16)
    return (code_values, scales)

def reference(base_weights, inner_weights, momentum):

    def add_replica(summed, replica_copy):
        deltas = base_weights - replica_copy.astype(jnp.float32)
        code_values, scales = encode(deltas)
        decoded = code_values.astype(jnp.float32) * scales[:, :, None]
        return (summed + decoded.reshape(deltas.shape), None)
    summed, unused = lax.scan(add_replica, jnp.zeros(base_weights.shape, jnp.float32), inner_weights)
    outer_grad = summed / REPLICAS
    grad_sq = jnp.sum(outer_grad * outer_grad)
    clip_factor = jnp.minimum(1.0, clip_rms / jnp.sqrt(grad_sq / (D * KVW) + epsilon))
    step_term = clip_factor * outer_grad
    new_momentum = outer_momentum * momentum + step_term
    new_base = base_weights - outer_rate * (step_term + outer_momentum * new_momentum)

    def blend_one(replica_copy):
        blended = blend_share * replica_copy.astype(jnp.float32) + (1.0 - blend_share) * new_base
        return blended.astype(jnp.bfloat16)
    new_inner = lax.map(blend_one, inner_weights)
    return (new_base, new_momentum, new_inner)
```

```python
import jax
import jax.numpy as jnp
from jax import lax
from jax.experimental import pallas as pl
from jax.experimental.pallas import tpu as pltpu
from jax.sharding import Mesh
from jax.sharding import PartitionSpec as P

D = 8192
KVW = 1024
BLOCK = 128
REPLICA = ("replica_0", "replica_1")
FSDP = ("fsdp_0", "fsdp_1", "fsdp_2")
FSDP_REPLICA = ("fsdp_0", "fsdp_1", "fsdp_2", "replica_0", "replica_1")
PLANE = ("replica_1", "fsdp_0")
RING = ("fsdp_1", "replica_0", "fsdp_2")

code_limit = 448.0
outer_rate = 0.7
outer_momentum = 0.9
blend_share = 0.5
clip_rms = 0.02
epsilon = 1e-06
smallest_normal = 0.015625

step_unit = 1024.0


def exchanged(blocks, axis):
    return lax.all_to_all(blocks, axis, split_axis=0, concat_axis=0, tiled=True)


def to_everyone(value, axis):
    copies = jnp.broadcast_to(value, (lax.axis_size(axis), *value.shape))
    return exchanged(copies, axis)


def smallest_scale(peaks):
    target = peaks * (1.0 / code_limit)
    spread = target * (2.0**23 + 1.0)
    scale = spread - (spread - target)
    scale = jnp.where(code_limit * scale < peaks, 2.0 * scale, scale)
    return jnp.where(code_limit * (0.5 * scale) >= peaks, 0.5 * scale, scale)


def encode_kernel(base_ref, inner_ref, decoded_ref):
    for at in range(0, base_ref.shape[1], BLOCK):
        columns = pl.ds(at, BLOCK)
        deltas = base_ref[:, columns] - inner_ref[:, columns].astype(jnp.float32)
        magnitude = jnp.abs(deltas)
        scale = smallest_scale(jnp.max(magnitude, axis=1, keepdims=True) + epsilon)
        beyond = deltas * (1.0 + 2.0**-23)
        spread = beyond * (2.0**20 + 1.0)
        normal = spread - (spread - beyond)
        anchor = scale * (1.5 * 2.0**14)
        small = (beyond + anchor) - anchor
        decoded = jnp.where(magnitude < scale * smallest_normal, small, normal)
        decoded_ref[:, columns] = decoded.astype(decoded_ref.dtype)


def decoded_deltas(base_weights, replica_copy):
    rows, columns = base_weights.shape
    tall = 64
    spec = pl.BlockSpec((tall, columns), lambda i: (i, 0))
    return pl.pallas_call(
        encode_kernel,
        grid=(rows // tall,),
        in_specs=[spec, spec],
        out_specs=spec,
        out_shape=jax.ShapeDtypeStruct((rows, columns), jnp.bfloat16),
        cost_estimate=pl.CostEstimate(
            flops=20 * rows * columns, bytes_accessed=8 * rows * columns, transcendentals=0
        ),
    )(base_weights, replica_copy)


def partial_squares(value):
    rows, columns = value.shape
    tiles = (value * value).reshape(rows // 8, 8, columns // 128, 128)
    return tiles.sum(axis=(0, 2))


def shards(base_weights, inner_weights, momentum):
    replicas = lax.axis_size(REPLICA)
    local_rows, columns = base_weights.shape
    owned_rows = local_rows // replicas
    replica_copy = inner_weights[0]
    decoded = decoded_deltas(base_weights, replica_copy)
    arrived = exchanged(decoded.reshape(replicas, owned_rows, columns), REPLICA)
    outer_grad = arrived.astype(jnp.float32).sum(axis=0) / replicas
    squares = to_everyone(partial_squares(outer_grad), PLANE).sum(axis=0)
    grad_sq = to_everyone(squares, RING).sum()
    clip_factor = jnp.minimum(1.0, clip_rms / jnp.sqrt(grad_sq / (D * KVW) + epsilon))
    step_term = clip_factor * outer_grad
    new_momentum = outer_momentum * momentum + step_term
    step = outer_rate * (step_term + outer_momentum * new_momentum)
    steps = to_everyone((step * step_unit).astype(jnp.float16), REPLICA)
    steps = steps.reshape(local_rows, columns).astype(jnp.float32) * (1.0 / step_unit)
    new_base = base_weights - steps
    blended = blend_share * replica_copy.astype(jnp.float32) + (1.0 - blend_share) * new_base
    return (new_base, new_momentum, blended.astype(jnp.bfloat16)[None])


def solution(mesh):
    torus = Mesh(
        mesh.devices.reshape(4, 4, 8, 2, 2),
        ("replica_0", "replica_1", "fsdp_0", "fsdp_1", "fsdp_2"),
    )
    return jax.shard_map(
        shards,
        mesh=torus,
        in_specs=(P(FSDP, None), P(REPLICA, FSDP, None), P(FSDP_REPLICA, None)),
        out_specs=(P(FSDP, None), P(FSDP_REPLICA, None), P(REPLICA, FSDP, None)),
        check_vma=False,
    )
```

```python
import jax
import jax.numpy as jnp
from jax import lax
from jax.experimental import pallas as pl
from jax.experimental.pallas import tpu as pltpu
from jax.sharding import Mesh
from jax.sharding import PartitionSpec as P

D = 8192
KVW = 1024
BLOCK = 128
REPLICA = ("replica_0", "replica_1")
FSDP = ("fsdp_0", "fsdp_1", "fsdp_2")
FSDP_REPLICA = ("fsdp_0", "fsdp_1", "fsdp_2", "replica_0", "replica_1")
code_limit = 448.0
outer_rate = 0.7
outer_momentum = 0.9
blend_share = 0.5
clip_rms = 0.02
epsilon = 1e-06
smallest_normal = 0.015625

grad_unit = 2048.0
momentum_unit = 32768.0


def exchanged(blocks, axis):
    return lax.all_to_all(blocks, axis, split_axis=0, concat_axis=0, tiled=True)


def to_everyone(value, axis):
    copies = jnp.broadcast_to(value, (lax.axis_size(axis), *value.shape))
    return exchanged(copies, axis)


def smallest_scale(peaks):
    target = peaks * (1.0 / code_limit)
    spread = target * (2.0**23 + 1.0)
    scale = spread - (spread - target)
    scale = jnp.where(code_limit * scale < peaks, 2.0 * scale, scale)
    return jnp.where(code_limit * (0.5 * scale) >= peaks, 0.5 * scale, scale)


def encode_kernel(base_ref, inner_ref, decoded_ref):
    for at in range(0, base_ref.shape[1], BLOCK):
        columns = pl.ds(at, BLOCK)
        deltas = base_ref[:, columns] - inner_ref[:, columns].astype(jnp.float32)
        magnitude = jnp.abs(deltas)
        scale = smallest_scale(jnp.max(magnitude, axis=1, keepdims=True) + epsilon)
        beyond = deltas * (1.0 + 2.0**-23)
        spread = beyond * (2.0**20 + 1.0)
        normal = spread - (spread - beyond)
        anchor = scale * (1.5 * 2.0**14)
        small = (beyond + anchor) - anchor
        decoded = jnp.where(magnitude < scale * smallest_normal, small, normal)
        decoded_ref[:, columns] = decoded.astype(decoded_ref.dtype)


def decoded_deltas(base_weights, replica_copy):
    rows, columns = base_weights.shape
    tall = 64
    spec = pl.BlockSpec((tall, columns), lambda i: (i, 0))
    return pl.pallas_call(
        encode_kernel,
        grid=(rows // tall,),
        in_specs=[spec, spec],
        out_specs=spec,
        out_shape=jax.ShapeDtypeStruct((rows, columns), jnp.bfloat16),
        cost_estimate=pl.CostEstimate(
            flops=20 * rows * columns, bytes_accessed=8 * rows * columns, transcendentals=0
        ),
    )(base_weights, replica_copy)


def partial_squares(value):
    rows, columns = value.shape
    tiles = (value * value).reshape(rows // 8, 8, columns // 128, 128)
    return tiles.sum(axis=(0, 2))


def in_half(value, unit):
    return (value.astype(jnp.float32) * unit).astype(jnp.float16)


def from_half(value, unit):
    return value.astype(jnp.float32) * (1.0 / unit)


def shards(base_weights, inner_weights, momentum):
    replicas = lax.axis_size(REPLICA)
    lines, line = lax.axis_size(REPLICA[0]), lax.axis_size(REPLICA[1])
    local_rows, columns = base_weights.shape
    owned_rows = local_rows // replicas
    share = columns // line
    replica_copy = inner_weights[0]

    decoded = decoded_deltas(base_weights, replica_copy)
    quarters = jnp.moveaxis(in_half(momentum, momentum_unit).reshape(owned_rows, line, share), 1, 0)
    quarters = jnp.broadcast_to(quarters, (lines, line, owned_rows, share))
    sent = jnp.concatenate(
        [
            in_half(decoded, grad_unit).reshape(replicas, owned_rows, columns),
            quarters.reshape(replicas, owned_rows, share),
        ],
        axis=2,
    )
    arrived = exchanged(sent, REPLICA)
    outer_grad = arrived[:, :, :columns].astype(jnp.float32).sum(axis=0) * (
        1.0 / (grad_unit * replicas)
    )
    quarter = from_half(arrived[:, :, columns:], momentum_unit).reshape(local_rows, share)
    all_quarters = lax.all_gather(quarter, REPLICA[1], axis=0, tiled=False)

    grads = to_everyone(in_half(outer_grad, grad_unit), REPLICA).reshape(local_rows, columns)
    squares = partial_squares(from_half(grads, grad_unit))
    all_squares = to_everyone(squares, FSDP)
    all_momentum = jnp.moveaxis(all_quarters, 0, 1).reshape(local_rows, columns)
    start = lax.optimization_barrier(
        base_weights - (outer_rate * outer_momentum * outer_momentum) * all_momentum
    )

    grad_sq = all_squares.sum()
    clip_factor = jnp.minimum(1.0, clip_rms / jnp.sqrt(grad_sq / (D * KVW) + epsilon))
    new_momentum = outer_momentum * momentum + clip_factor * outer_grad
    rate = (outer_rate * (1.0 + outer_momentum) / grad_unit) * clip_factor
    new_base = start - rate * grads.astype(jnp.float32)
    blended = blend_share * replica_copy.astype(jnp.float32) + (1.0 - blend_share) * new_base
    return (new_base, new_momentum, blended.astype(jnp.bfloat16)[None])


def solution(mesh):
    torus = Mesh(
        mesh.devices.reshape(4, 4, 8, 2, 2),
        ("replica_0", "replica_1", "fsdp_0", "fsdp_1", "fsdp_2"),
    )
    return jax.shard_map(
        shards,
        mesh=torus,
        in_specs=(P(FSDP, None), P(REPLICA, FSDP, None), P(FSDP_REPLICA, None)),
        out_specs=(P(FSDP, None), P(FSDP_REPLICA, None), P(REPLICA, FSDP, None)),
        check_vma=False,
    )
```

```python
import jax
import jax.numpy as jnp
from jax import lax
from jax.experimental import pallas as pl
from jax.experimental.pallas import tpu as pltpu
from jax.sharding import Mesh
from jax.sharding import PartitionSpec as P

D = 8192
KVW = 1024
BLOCK = 128
REPLICA = ("replica_0", "replica_1")
FSDP = ("fsdp_0", "fsdp_1", "fsdp_2")
FSDP_REPLICA = ("fsdp_0", "fsdp_1", "fsdp_2", "replica_0", "replica_1")
PLANE = ("replica_1", "fsdp_0")
RING = ("fsdp_1", "replica_0", "fsdp_2")
code_limit = 448.0
outer_rate = 0.7
outer_momentum = 0.9
blend_share = 0.5
clip_rms = 0.02
epsilon = 1e-06
smallest_normal = 0.015625

grad_unit = 2048.0
momentum_unit = 32768.0


def exchanged(blocks, axis):
    return lax.all_to_all(blocks, axis, split_axis=0, concat_axis=0, tiled=True)


def to_everyone(value, axis):
    copies = jnp.broadcast_to(value, (lax.axis_size(axis), *value.shape))
    return exchanged(copies, axis)


def smallest_scale(peaks):
    target = peaks * (1.0 / code_limit)
    spread = target * (2.0**23 + 1.0)
    scale = spread - (spread - target)
    scale = jnp.where(code_limit * scale < peaks, 2.0 * scale, scale)
    return jnp.where(code_limit * (0.5 * scale) >= peaks, 0.5 * scale, scale)


def encode_kernel(base_ref, inner_ref, decoded_ref):
    for at in range(0, base_ref.shape[1], BLOCK):
        columns = pl.ds(at, BLOCK)
        deltas = base_ref[:, columns] - inner_ref[:, columns].astype(jnp.float32)
        magnitude = jnp.abs(deltas)
        scale = smallest_scale(jnp.max(magnitude, axis=1, keepdims=True) + epsilon)
        beyond = deltas * (1.0 + 2.0**-23)
        spread = beyond * (2.0**20 + 1.0)
        normal = spread - (spread - beyond)
        anchor = scale * (1.5 * 2.0**14)
        small = (beyond + anchor) - anchor
        decoded = jnp.where(magnitude < scale * smallest_normal, small, normal)
        decoded_ref[:, columns] = decoded.astype(decoded_ref.dtype)


def decoded_deltas(base_weights, replica_copy):
    rows, columns = base_weights.shape
    tall = 64
    spec = pl.BlockSpec((tall, columns), lambda i: (i, 0))
    return pl.pallas_call(
        encode_kernel,
        grid=(rows // tall,),
        in_specs=[spec, spec],
        out_specs=spec,
        out_shape=jax.ShapeDtypeStruct((rows, columns), jnp.bfloat16),
        cost_estimate=pl.CostEstimate(
            flops=20 * rows * columns, bytes_accessed=8 * rows * columns, transcendentals=0
        ),
    )(base_weights, replica_copy)


def partial_squares(value):
    rows, columns = value.shape
    tiles = (value * value).reshape(rows // 8, 8, columns // 128, 128)
    return tiles.sum(axis=(0, 2))


def in_half(value, unit):
    return (value.astype(jnp.float32) * unit).astype(jnp.float16)


def from_half(value, unit):
    return value.astype(jnp.float32) * (1.0 / unit)


def swapped(value, axis, bit):
    return lax.ppermute(value, axis, [(i, i ^ bit) for i in range(lax.axis_size(axis))])


def gathered(value, axis):
    place = lax.axis_index(axis)
    upper, odd = place >= 2, (place & 1) == 1
    other = swapped(value, axis, 2)
    halves = jnp.stack([jnp.where(upper, other, value), jnp.where(upper, value, other)])
    other = swapped(halves, axis, 1)
    evens, odds = jnp.where(odd, other, halves), jnp.where(odd, halves, other)
    return jnp.stack([evens[0], odds[0], evens[1], odds[1]])


def beside(task, value):
    shape = jax.eval_shape(task, value)
    held = value.reshape(-1)[0].astype(jnp.float32) < 1e30
    return lax.cond(held, task, lambda v: jnp.zeros(shape.shape, shape.dtype), value)


def in_rows(blocks):
    return jnp.swapaxes(blocks, 0, 1).reshape(-1, blocks.shape[-1])


def shards(base_weights, inner_weights, momentum):
    replicas = lax.axis_size(REPLICA)
    local_rows, columns = base_weights.shape
    owned_rows = local_rows // replicas
    replica_copy = inner_weights[0]
    together = lax.optimization_barrier

    decoded, momenta = together(
        (decoded_deltas(base_weights, replica_copy), in_half(momentum, momentum_unit))
    )
    arrived = exchanged(decoded.reshape(replicas, owned_rows, columns), REPLICA)
    momenta = beside(lambda v: gathered(gathered(v, REPLICA[0]), REPLICA[1]), momenta)
    arrived, momenta = together((arrived, momenta))
    outer_grad = arrived.astype(jnp.float32).sum(axis=0) / replicas

    squares, grads = together((partial_squares(outer_grad), in_half(outer_grad, grad_unit)))
    squares = to_everyone(squares, PLANE)
    grads = beside(lambda v: gathered(v, REPLICA[0]), grads)
    squares, grads = together((squares, grads))
    squares, grads = together((squares.sum(axis=0), grads))
    squares = to_everyone(squares, RING)
    grads = beside(lambda v: gathered(v, REPLICA[1]), grads)
    squares, grads = together((squares, grads))

    grad_sq = squares.sum()
    clip_factor = jnp.minimum(1.0, clip_rms / jnp.sqrt(grad_sq / (D * KVW) + epsilon))
    new_momentum = outer_momentum * momentum + clip_factor * outer_grad
    start = base_weights - (
        outer_rate * outer_momentum * outer_momentum / momentum_unit
    ) * in_rows(momenta).astype(jnp.float32)
    rate = (outer_rate * (1.0 + outer_momentum) / grad_unit) * clip_factor
    new_base = start - rate * in_rows(grads).astype(jnp.float32)
    blended = blend_share * replica_copy.astype(jnp.float32) + (1.0 - blend_share) * new_base
    return (new_base, new_momentum, blended.astype(jnp.bfloat16)[None])


def solution(mesh):
    torus = Mesh(
        mesh.devices.reshape(4, 4, 8, 2, 2),
        ("replica_0", "replica_1", "fsdp_0", "fsdp_1", "fsdp_2"),
    )
    return jax.shard_map(
        shards,
        mesh=torus,
        in_specs=(P(FSDP, None), P(REPLICA, FSDP, None), P(FSDP_REPLICA, None)),
        out_specs=(P(FSDP, None), P(FSDP_REPLICA, None), P(REPLICA, FSDP, None)),
        check_vma=False,
    )
```

```python
import jax
import jax.numpy as jnp
from jax import lax
from jax.experimental import pallas as pl
from jax.experimental.pallas import tpu as pltpu
from jax.sharding import Mesh
from jax.sharding import PartitionSpec as P

D = 8192
KVW = 1024
BLOCK = 128
REPLICA = ("replica_0", "replica_1")
FSDP = ("fsdp_0", "fsdp_1", "fsdp_2")
FSDP_REPLICA = ("fsdp_0", "fsdp_1", "fsdp_2", "replica_0", "replica_1")
code_limit = 448.0
outer_rate = 0.7
outer_momentum = 0.9
blend_share = 0.5
clip_rms = 0.02
epsilon = 1e-06
smallest_normal = 0.015625

grad_unit = 2048.0
momentum_unit = 32768.0


def exchanged(blocks, axis):
    return lax.all_to_all(blocks, axis, split_axis=0, concat_axis=0, tiled=True)


def to_everyone(value, axis):
    copies = jnp.broadcast_to(value, (lax.axis_size(axis), *value.shape))
    return exchanged(copies, axis)


def smallest_scale(peaks):
    target = peaks * (1.0 / code_limit)
    spread = target * (2.0**23 + 1.0)
    scale = spread - (spread - target)
    scale = jnp.where(code_limit * scale < peaks, 2.0 * scale, scale)
    return jnp.where(code_limit * (0.5 * scale) >= peaks, 0.5 * scale, scale)


def encode_kernel(base_ref, inner_ref, decoded_ref):
    for at in range(0, base_ref.shape[1], BLOCK):
        columns = pl.ds(at, BLOCK)
        deltas = base_ref[:, columns] - inner_ref[:, columns].astype(jnp.float32)
        magnitude = jnp.abs(deltas)
        scale = smallest_scale(jnp.max(magnitude, axis=1, keepdims=True) + epsilon)
        beyond = deltas * (1.0 + 2.0**-23)
        spread = beyond * (2.0**20 + 1.0)
        normal = spread - (spread - beyond)
        anchor = scale * (1.5 * 2.0**14)
        small = (beyond + anchor) - anchor
        decoded = jnp.where(magnitude < scale * smallest_normal, small, normal)
        decoded_ref[:, columns] = decoded.astype(decoded_ref.dtype)


def decoded_deltas(base_weights, replica_copy):
    rows, columns = base_weights.shape
    tall = 64
    spec = pl.BlockSpec((tall, columns), lambda i: (i, 0))
    return pl.pallas_call(
        encode_kernel,
        grid=(rows // tall,),
        in_specs=[spec, spec],
        out_specs=spec,
        out_shape=jax.ShapeDtypeStruct((rows, columns), jnp.bfloat16),
        cost_estimate=pl.CostEstimate(
            flops=20 * rows * columns, bytes_accessed=8 * rows * columns, transcendentals=0
        ),
    )(base_weights, replica_copy)


def partial_squares(value):
    rows, columns = value.shape
    tiles = (value * value).reshape(rows // 8, 8, columns // 128, 128)
    return tiles.sum(axis=(0, 2))


def in_half(value, unit):
    return (value.astype(jnp.float32) * unit).astype(jnp.float16)


def from_half(value, unit):
    return value.astype(jnp.float32) * (1.0 / unit)


def gathered(value, axis):
    size, place = lax.axis_size(axis), lax.axis_index(axis)
    seen = [value] + [
        lax.ppermute(value, axis, [(i, (i + far) % size) for i in range(size)])
        for far in range(1, size)
    ]
    ordered = []
    for at in range(size):
        block = seen[0]
        for far in range(1, size):
            block = jnp.where(lax.rem(place - at + size, size) == far, seen[far], block)
        ordered.append(block)
    return jnp.stack(ordered)


def beside(task, value):
    shape = jax.eval_shape(task, value)
    held = value.reshape(-1)[0].astype(jnp.float32) < 1e30
    return lax.cond(held, task, lambda v: jnp.zeros(shape.shape, shape.dtype), value)


def shards(base_weights, inner_weights, momentum):
    replicas = lax.axis_size(REPLICA)
    local_rows, columns = base_weights.shape
    owned_rows = local_rows // replicas
    replica_copy = inner_weights[0]
    together = lax.optimization_barrier

    decoded, momenta = together(
        (decoded_deltas(base_weights, replica_copy), in_half(momentum, momentum_unit))
    )
    arrived = exchanged(decoded.reshape(replicas, owned_rows, columns), REPLICA)
    momenta = beside(lambda v: gathered(v, REPLICA[0]), momenta)
    arrived, momenta = together((arrived, momenta))
    outer_grad = arrived.astype(jnp.float32).sum(axis=0) / replicas

    grads, momenta = together((in_half(outer_grad, grad_unit), momenta))
    grads = to_everyone(grads, REPLICA).reshape(local_rows, columns)
    momenta = beside(lambda v: gathered(v, REPLICA[1]), momenta)
    grads, momenta = together((grads, momenta))

    squares = to_everyone(partial_squares(from_half(grads, grad_unit)), FSDP)
    momenta = jnp.swapaxes(momenta, 0, 1).reshape(local_rows, columns)
    start = together(
        base_weights
        - (outer_rate * outer_momentum * outer_momentum) * from_half(momenta, momentum_unit)
    )
    grad_sq = squares.sum()
    clip_factor = jnp.minimum(1.0, clip_rms / jnp.sqrt(grad_sq / (D * KVW) + epsilon))
    new_momentum = outer_momentum * momentum + clip_factor * outer_grad
    rate = (outer_rate * (1.0 + outer_momentum) / grad_unit) * clip_factor
    new_base = start - rate * grads.astype(jnp.float32)
    blended = blend_share * replica_copy.astype(jnp.float32) + (1.0 - blend_share) * new_base
    return (new_base, new_momentum, blended.astype(jnp.bfloat16)[None])


def solution(mesh):
    torus = Mesh(
        mesh.devices.reshape(4, 4, 8, 2, 2),
        ("replica_0", "replica_1", "fsdp_0", "fsdp_1", "fsdp_2"),
    )
    return jax.shard_map(
        shards,
        mesh=torus,
        in_specs=(P(FSDP, None), P(REPLICA, FSDP, None), P(FSDP_REPLICA, None)),
        out_specs=(P(FSDP, None), P(FSDP_REPLICA, None), P(REPLICA, FSDP, None)),
        check_vma=False,
    )
```

```python
import jax
import jax.numpy as jnp
from jax import lax
from jax.experimental import pallas as pl
from jax.experimental.pallas import tpu as pltpu
from jax.sharding import Mesh
from jax.sharding import PartitionSpec as P

D = 8192
KVW = 1024
BLOCK = 128
REPLICA = ("replica_0", "replica_1")
FSDP = ("fsdp_0", "fsdp_1", "fsdp_2")
FSDP_REPLICA = ("fsdp_0", "fsdp_1", "fsdp_2", "replica_0", "replica_1")
code_limit = 448.0
outer_rate = 0.7
outer_momentum = 0.9
blend_share = 0.5
clip_rms = 0.02
epsilon = 1e-06
smallest_normal = 0.015625

sum_unit = 512.0
grad_unit = 2048.0
momentum_unit = 32768.0


def exchanged(blocks, axis):
    return lax.all_to_all(blocks, axis, split_axis=0, concat_axis=0, tiled=True)


def to_everyone(value, axis):
    copies = jnp.broadcast_to(value, (lax.axis_size(axis), *value.shape))
    return exchanged(copies, axis)


def smallest_scale(peaks):
    target = peaks * (1.0 / code_limit)
    spread = target * (2.0**23 + 1.0)
    scale = spread - (spread - target)
    scale = jnp.where(code_limit * scale < peaks, 2.0 * scale, scale)
    return jnp.where(code_limit * (0.5 * scale) >= peaks, 0.5 * scale, scale)


def encoded(base_block, inner_block):
    deltas = base_block - inner_block.astype(jnp.float32)
    magnitude = jnp.abs(deltas)
    scale = smallest_scale(jnp.max(magnitude, axis=1, keepdims=True) + epsilon)
    beyond = deltas * (1.0 + 2.0**-23)
    spread = beyond * (2.0**20 + 1.0)
    normal = spread - (spread - beyond)
    anchor = scale * (1.5 * 2.0**14)
    small = (beyond + anchor) - anchor
    return jnp.where(magnitude < scale * smallest_normal, small, normal)


def encode_kernel(base_ref, inner_ref, decoded_ref):
    across, along, rows, columns = decoded_ref.shape
    for at in range(0, columns, BLOCK):
        lanes = pl.ds(at, BLOCK)
        decoded = encoded(base_ref[:, lanes], inner_ref[:, lanes]).astype(decoded_ref.dtype)
        for y in range(along):
            for x in range(across):
                first = (y * across + x) * rows
                decoded_ref[x, y, :, lanes] = decoded[first : first + rows]


def decoded_deltas(base_weights, replica_copy, along, across):
    rows, columns = base_weights.shape
    steps = 2
    tall = rows // steps
    owned_rows = rows // (along * across)
    spec = pl.BlockSpec((tall, columns), lambda i: (i, 0))
    return pl.pallas_call(
        encode_kernel,
        grid=(steps,),
        in_specs=[spec, spec],
        out_specs=pl.BlockSpec(
            (across, along // steps, owned_rows, columns), lambda i: (0, i, 0, 0)
        ),
        out_shape=jax.ShapeDtypeStruct((across, along, owned_rows, columns), jnp.bfloat16),
        cost_estimate=pl.CostEstimate(
            flops=20 * rows * columns, bytes_accessed=8 * rows * columns, transcendentals=0
        ),
    )(base_weights, replica_copy)


def partial_squares(value):
    rows, columns = value.shape
    tiles = (value * value).reshape(rows // 8, 8, columns // 128, 128)
    return tiles.sum(axis=(0, 2))


def in_half(value, unit):
    return (value.astype(jnp.float32) * unit).astype(jnp.float16)


def from_half(value, unit):
    return value.astype(jnp.float32) * (1.0 / unit)


def shards(base_weights, inner_weights, momentum):
    along, across = lax.axis_size(REPLICA[0]), lax.axis_size(REPLICA[1])
    replicas = along * across
    local_rows, columns = base_weights.shape
    owned_rows = local_rows // replicas
    line_rows = along * owned_rows
    replica_copy = inner_weights[0]

    decoded = decoded_deltas(base_weights, replica_copy, along, across)
    arrived = exchanged(decoded.reshape(across, line_rows, columns), REPLICA[1])
    sums = arrived.astype(jnp.float32).sum(axis=0)

    sent = jnp.concatenate([in_half(sums, sum_unit), in_half(momentum, momentum_unit)])
    arrived = to_everyone(sent, REPLICA[0])
    outer_grad = arrived[:, :line_rows].astype(jnp.float32).sum(axis=0) * (
        1.0 / (sum_unit * replicas)
    )
    momenta = arrived[:, line_rows:].reshape(line_rows, columns)
    owned_grad = lax.dynamic_slice_in_dim(
        outer_grad, lax.axis_index(REPLICA[0]) * owned_rows, owned_rows, 0
    )

    everyones = to_everyone(jnp.stack([in_half(outer_grad, grad_unit), momenta]), REPLICA[1])
    everyones = everyones.reshape(across, 2, along, owned_rows, columns)
    grads, momenta = jnp.moveaxis(everyones, (1, 2), (0, 1)).reshape(2, local_rows, columns)

    squares = to_everyone(partial_squares(from_half(everyones[:, 0].reshape(local_rows, columns), grad_unit)), FSDP)
    start = lax.optimization_barrier(
        base_weights
        - (outer_rate * outer_momentum * outer_momentum) * from_half(momenta, momentum_unit)
    )
    grad_sq = squares.sum()
    clip_factor = jnp.minimum(1.0, clip_rms / jnp.sqrt(grad_sq / (D * KVW) + epsilon))
    new_momentum = outer_momentum * momentum + clip_factor * owned_grad
    rate = (outer_rate * (1.0 + outer_momentum) / grad_unit) * clip_factor
    new_base = start - rate * grads.astype(jnp.float32)
    blended = blend_share * replica_copy.astype(jnp.float32) + (1.0 - blend_share) * new_base
    return (new_base, new_momentum, blended.astype(jnp.bfloat16)[None])


def solution(mesh):
    torus = Mesh(
        mesh.devices.reshape(4, 4, 8, 2, 2),
        ("replica_0", "replica_1", "fsdp_0", "fsdp_1", "fsdp_2"),
    )
    return jax.shard_map(
        shards,
        mesh=torus,
        in_specs=(P(FSDP, None), P(REPLICA, FSDP, None), P(FSDP_REPLICA, None)),
        out_specs=(P(FSDP, None), P(FSDP_REPLICA, None), P(REPLICA, FSDP, None)),
        check_vma=False,
    )
```

```python
import jax
import jax.numpy as jnp
from jax import lax
from jax.experimental import pallas as pl
from jax.experimental.pallas import tpu as pltpu
from jax.sharding import Mesh
from jax.sharding import PartitionSpec as P

D = 8192
KVW = 1024
BLOCK = 128
REPLICA = ("replica_0", "replica_1")
FSDP = ("fsdp_0", "fsdp_1", "fsdp_2")
FSDP_REPLICA = ("fsdp_0", "fsdp_1", "fsdp_2", "replica_0", "replica_1")
PLANE = ("replica_1", "fsdp_0")
RING = ("fsdp_1", "replica_0", "fsdp_2")

code_limit = 448.0
outer_rate = 0.7
outer_momentum = 0.9
blend_share = 0.5
clip_rms = 0.02
epsilon = 1e-06
smallest_normal = 0.015625

step_unit = 1024.0


def exchanged(blocks, axis):
    return lax.all_to_all(blocks, axis, split_axis=0, concat_axis=0, tiled=True)


def to_everyone(value, axis):
    copies = jnp.broadcast_to(value, (lax.axis_size(axis), *value.shape))
    return exchanged(copies, axis)


def smallest_scale(peaks):
    target = peaks * (1.0 / code_limit)
    spread = target * (2.0**23 + 1.0)
    scale = spread - (spread - target)
    scale = jnp.where(code_limit * scale < peaks, 2.0 * scale, scale)
    return jnp.where(code_limit * (0.5 * scale) >= peaks, 0.5 * scale, scale)


def encode_kernel(base_ref, inner_ref, decoded_ref):
    for at in range(0, base_ref.shape[1], BLOCK):
        columns = pl.ds(at, BLOCK)
        deltas = base_ref[:, columns] - inner_ref[:, columns].astype(jnp.float32)
        magnitude = jnp.abs(deltas)
        scale = smallest_scale(jnp.max(magnitude, axis=1, keepdims=True) + epsilon)
        beyond = deltas * (1.0 + 2.0**-23)
        spread = beyond * (2.0**20 + 1.0)
        normal = spread - (spread - beyond)
        anchor = scale * (1.5 * 2.0**14)
        small = (beyond + anchor) - anchor
        decoded = jnp.where(magnitude < scale * smallest_normal, small, normal)
        decoded_ref[:, columns] = decoded.astype(decoded_ref.dtype)


def decoded_deltas(base_weights, replica_copy):
    rows, columns = base_weights.shape
    tall = rows // 2
    spec = pl.BlockSpec((tall, columns), lambda i: (i, 0))
    return pl.pallas_call(
        encode_kernel,
        grid=(rows // tall,),
        in_specs=[spec, spec],
        out_specs=spec,
        out_shape=jax.ShapeDtypeStruct((rows, columns), jnp.bfloat16),
        cost_estimate=pl.CostEstimate(
            flops=20 * rows * columns, bytes_accessed=8 * rows * columns, transcendentals=0
        ),
    )(base_weights, replica_copy)


def partial_squares(value):
    rows, columns = value.shape
    tiles = (value * value).reshape(rows // 8, 8, columns // 128, 128)
    return tiles.sum(axis=(0, 2))


def shards(base_weights, inner_weights, momentum):
    replicas = lax.axis_size(REPLICA)
    local_rows, columns = base_weights.shape
    owned_rows = local_rows // replicas
    replica_copy = inner_weights[0]
    decoded = decoded_deltas(base_weights, replica_copy)
    arrived = exchanged(decoded.reshape(replicas, owned_rows, columns), REPLICA)
    blended = blend_share * replica_copy.astype(jnp.float32) + (1.0 - blend_share) * base_weights
    arrived, blended = lax.optimization_barrier((arrived, blended))
    outer_grad = arrived.astype(jnp.float32).sum(axis=0) / replicas
    squares = to_everyone(partial_squares(outer_grad), PLANE).sum(axis=0)
    grad_sq = to_everyone(squares, RING).sum()
    clip_factor = jnp.minimum(1.0, clip_rms / jnp.sqrt(grad_sq / (D * KVW) + epsilon))
    step_term = clip_factor * outer_grad
    new_momentum = outer_momentum * momentum + step_term
    step = outer_rate * (step_term + outer_momentum * new_momentum)
    steps = to_everyone((step * step_unit).astype(jnp.float16), REPLICA)
    steps = steps.reshape(local_rows, columns).astype(jnp.float32) * (1.0 / step_unit)
    new_inner = (blended - (1.0 - blend_share) * steps).astype(jnp.bfloat16)
    return (base_weights - steps, new_momentum, new_inner[None])


def solution(mesh):
    torus = Mesh(
        mesh.devices.reshape(4, 4, 8, 2, 2),
        ("replica_0", "replica_1", "fsdp_0", "fsdp_1", "fsdp_2"),
    )
    return jax.shard_map(
        shards,
        mesh=torus,
        in_specs=(P(FSDP, None), P(REPLICA, FSDP, None), P(FSDP_REPLICA, None)),
        out_specs=(P(FSDP, None), P(FSDP_REPLICA, None), P(REPLICA, FSDP, None)),
        check_vma=False,
    )
```

```python
import jax
import jax.numpy as jnp
from jax import lax
from jax.experimental import pallas as pl
from jax.experimental.pallas import tpu as pltpu
from jax.sharding import Mesh
from jax.sharding import PartitionSpec as P

D = 8192
KVW = 1024
BLOCK = 128
REPLICA = ("replica_0", "replica_1")
FSDP = ("fsdp_0", "fsdp_1", "fsdp_2")
FSDP_REPLICA = ("fsdp_0", "fsdp_1", "fsdp_2", "replica_0", "replica_1")
code_limit = 448.0
outer_rate = 0.7
outer_momentum = 0.9
blend_share = 0.5
clip_rms = 0.02
epsilon = 1e-06
smallest_normal = 0.015625

grad_unit = 2048.0
momentum_unit = 32768.0


def exchanged(blocks, axis):
    return lax.all_to_all(blocks, axis, split_axis=0, concat_axis=0, tiled=True)


def to_everyone(value, axis):
    copies = jnp.broadcast_to(value, (lax.axis_size(axis), *value.shape))
    return exchanged(copies, axis)


def smallest_scale(peaks):
    target = peaks * (1.0 / code_limit)
    spread = target * (2.0**23 + 1.0)
    scale = spread - (spread - target)
    scale = jnp.where(code_limit * scale < peaks, 2.0 * scale, scale)
    return jnp.where(code_limit * (0.5 * scale) >= peaks, 0.5 * scale, scale)


def encode_kernel(base_ref, inner_ref, decoded_ref):
    for at in range(0, base_ref.shape[1], BLOCK):
        columns = pl.ds(at, BLOCK)
        deltas = base_ref[:, columns] - inner_ref[:, columns].astype(jnp.float32)
        magnitude = jnp.abs(deltas)
        scale = smallest_scale(jnp.max(magnitude, axis=1, keepdims=True) + epsilon)
        beyond = deltas * (1.0 + 2.0**-23)
        spread = beyond * (2.0**20 + 1.0)
        normal = spread - (spread - beyond)
        anchor = scale * (1.5 * 2.0**14)
        small = (beyond + anchor) - anchor
        decoded = jnp.where(magnitude < scale * smallest_normal, small, normal)
        decoded_ref[:, columns] = decoded.astype(decoded_ref.dtype)


def decoded_deltas(base_weights, replica_copy):
    rows, columns = base_weights.shape
    tall = rows // 2
    spec = pl.BlockSpec((tall, columns), lambda i: (i, 0))
    return pl.pallas_call(
        encode_kernel,
        grid=(rows // tall,),
        in_specs=[spec, spec],
        out_specs=spec,
        out_shape=jax.ShapeDtypeStruct((rows, columns), jnp.bfloat16),
        cost_estimate=pl.CostEstimate(
            flops=20 * rows * columns, bytes_accessed=8 * rows * columns, transcendentals=0
        ),
    )(base_weights, replica_copy)


def partial_squares(value):
    rows, columns = value.shape
    tiles = (value * value).reshape(rows // 8, 8, columns // 128, 128)
    return tiles.sum(axis=(0, 2))


def in_half(value, unit):
    return (value.astype(jnp.float32) * unit).astype(jnp.float16)


def from_half(value, unit):
    return value.astype(jnp.float32) * (1.0 / unit)


def gathered(value, axis):
    return lax.all_gather(value, axis, axis=0, tiled=False)


def shards(base_weights, inner_weights, momentum):
    replicas = lax.axis_size(REPLICA)
    local_rows, columns = base_weights.shape
    owned_rows = local_rows // replicas
    replica_copy = inner_weights[0]
    together = lax.optimization_barrier

    decoded, momenta = together((decoded_deltas(base_weights, replica_copy), momentum))
    arrived = exchanged(decoded.reshape(replicas, owned_rows, columns), REPLICA)
    momenta = gathered(in_half(momenta, momentum_unit), REPLICA[0])
    arrived, momenta = together((arrived, momenta))
    outer_grad = arrived.astype(jnp.float32).sum(axis=0) / replicas

    grads, momenta = together((in_half(outer_grad, grad_unit), momenta))
    grads = to_everyone(grads, REPLICA).reshape(local_rows, columns)
    momenta = gathered(momenta, REPLICA[1])
    momenta = jnp.swapaxes(momenta, 0, 1).reshape(local_rows, columns)
    start = base_weights - (outer_rate * outer_momentum * outer_momentum) * from_half(
        momenta, momentum_unit
    )
    grads, start = together((grads, start))

    squares = to_everyone(partial_squares(from_half(grads, grad_unit)), FSDP)
    grad_sq = squares.sum()
    clip_factor = jnp.minimum(1.0, clip_rms / jnp.sqrt(grad_sq / (D * KVW) + epsilon))
    new_momentum = outer_momentum * momentum + clip_factor * outer_grad
    rate = (outer_rate * (1.0 + outer_momentum) / grad_unit) * clip_factor
    new_base = start - rate * grads.astype(jnp.float32)
    blended = blend_share * replica_copy.astype(jnp.float32) + (1.0 - blend_share) * new_base
    return (new_base, new_momentum, blended.astype(jnp.bfloat16)[None])


def solution(mesh):
    torus = Mesh(
        mesh.devices.reshape(4, 4, 8, 2, 2),
        ("replica_0", "replica_1", "fsdp_0", "fsdp_1", "fsdp_2"),
    )
    return jax.shard_map(
        shards,
        mesh=torus,
        in_specs=(P(FSDP, None), P(REPLICA, FSDP, None), P(FSDP_REPLICA, None)),
        out_specs=(P(FSDP, None), P(FSDP_REPLICA, None), P(REPLICA, FSDP, None)),
        check_vma=False,
    )
```

```python
import jax
import jax.numpy as jnp
from jax import lax
from jax.experimental import pallas as pl
from jax.experimental.pallas import tpu as pltpu
from jax.sharding import Mesh
from jax.sharding import PartitionSpec as P

D = 8192
KVW = 1024
BLOCK = 128
REPLICA = ("replica_0", "replica_1")
FSDP = ("fsdp_0", "fsdp_1", "fsdp_2")
FSDP_REPLICA = ("fsdp_0", "fsdp_1", "fsdp_2", "replica_0", "replica_1")
RING = ("fsdp_1", "replica_0", "fsdp_2")
PLANE = ("replica_1", "fsdp_0")

code_limit = 448.0
outer_rate = 0.7
outer_momentum = 0.9
blend_share = 0.5
clip_rms = 0.02
epsilon = 1e-06
smallest_normal = 0.015625

step_unit = 1024.0


def exchanged(blocks, axis):
    return lax.all_to_all(blocks, axis, split_axis=0, concat_axis=0, tiled=True)


def to_everyone(value, axis):
    copies = jnp.broadcast_to(value, (lax.axis_size(axis), *value.shape))
    return exchanged(copies, axis)


def smallest_scale(peaks):
    target = peaks * (1.0 / code_limit)
    spread = target * (2.0**23 + 1.0)
    scale = spread - (spread - target)
    scale = jnp.where(code_limit * scale < peaks, 2.0 * scale, scale)
    return jnp.where(code_limit * (0.5 * scale) >= peaks, 0.5 * scale, scale)


def encode_kernel(base_ref, inner_ref, decoded_ref):
    for at in range(0, base_ref.shape[1], BLOCK):
        columns = pl.ds(at, BLOCK)
        deltas = base_ref[:, columns] - inner_ref[:, columns].astype(jnp.float32)
        magnitude = jnp.abs(deltas)
        scale = smallest_scale(jnp.max(magnitude, axis=1, keepdims=True) + epsilon)
        beyond = deltas * (1.0 + 2.0**-23)
        spread = beyond * (2.0**20 + 1.0)
        normal = spread - (spread - beyond)
        anchor = scale * (1.5 * 2.0**14)
        small = (beyond + anchor) - anchor
        decoded = jnp.where(magnitude < scale * smallest_normal, small, normal)
        decoded_ref[:, columns] = decoded.astype(decoded_ref.dtype)


def decoded_deltas(base_weights, replica_copy):
    rows, columns = base_weights.shape
    tall = rows // 2
    spec = pl.BlockSpec((tall, columns), lambda i: (i, 0))
    return pl.pallas_call(
        encode_kernel,
        grid=(rows // tall,),
        in_specs=[spec, spec],
        out_specs=spec,
        out_shape=jax.ShapeDtypeStruct((rows, columns), jnp.bfloat16),
        cost_estimate=pl.CostEstimate(
            flops=20 * rows * columns, bytes_accessed=8 * rows * columns, transcendentals=0
        ),
    )(base_weights, replica_copy)


def lane_squares(value):
    rows, columns = value.shape
    tiles = (value * value).reshape(rows // 8, 8, columns // 128, 128)
    return tiles.sum(axis=(0, 1, 2))[None]


def lane_total(lanes, columns):
    ones = jnp.ones((lanes.shape[1], columns), lanes.dtype)
    return lax.dot(lanes, ones, precision=lax.Precision.HIGHEST)


def shards(base_weights, inner_weights, momentum):
    replicas = lax.axis_size(REPLICA)
    local_rows, columns = base_weights.shape
    owned_rows = local_rows // replicas
    replica_copy = inner_weights[0]
    decoded = decoded_deltas(base_weights, replica_copy)
    arrived = exchanged(decoded.reshape(replicas, owned_rows, columns), REPLICA)
    blended = blend_share * replica_copy.astype(jnp.float32) + (1.0 - blend_share) * base_weights
    arrived, blended = lax.optimization_barrier((arrived, blended))
    outer_grad = arrived.astype(jnp.float32).sum(axis=0) / replicas
    squares = to_everyone(lane_squares(outer_grad), RING).sum(axis=0)
    squares = to_everyone(squares, PLANE).sum(axis=0)
    grad_sq = lane_total(squares, columns)
    clip_factor = jnp.minimum(1.0, clip_rms / jnp.sqrt(grad_sq / (D * KVW) + epsilon))
    step_term = clip_factor * outer_grad
    new_momentum = outer_momentum * momentum + step_term
    step = outer_rate * (step_term + outer_momentum * new_momentum)
    steps = to_everyone((step * step_unit).astype(jnp.float16), REPLICA)
    steps = lax.optimization_barrier(steps.reshape(local_rows, columns))
    steps = steps.astype(jnp.float32) * (1.0 / step_unit)
    new_inner = (blended - (1.0 - blend_share) * steps).astype(jnp.bfloat16)
    return (base_weights - steps, new_momentum, new_inner[None])


def solution(mesh):
    torus = Mesh(
        mesh.devices.reshape(4, 4, 8, 2, 2),
        ("replica_0", "replica_1", "fsdp_0", "fsdp_1", "fsdp_2"),
    )
    return jax.shard_map(
        shards,
        mesh=torus,
        in_specs=(P(FSDP, None), P(REPLICA, FSDP, None), P(FSDP_REPLICA, None)),
        out_specs=(P(FSDP, None), P(FSDP_REPLICA, None), P(REPLICA, FSDP, None)),
        check_vma=False,
    )
```

```python
import jax
import jax.numpy as jnp
from jax import lax
from jax.experimental import pallas as pl
from jax.experimental.pallas import tpu as pltpu
from jax.sharding import Mesh
from jax.sharding import PartitionSpec as P

D = 8192
KVW = 1024
BLOCK = 128
REPLICA = ("replica_0", "replica_1")
FSDP = ("fsdp_0", "fsdp_1", "fsdp_2")
FSDP_REPLICA = ("fsdp_0", "fsdp_1", "fsdp_2", "replica_0", "replica_1")
RING = ("fsdp_1", "replica_0", "fsdp_2")
PLANE = ("replica_1", "fsdp_0")

code_limit = 448.0
outer_rate = 0.7
outer_momentum = 0.9
blend_share = 0.5
clip_rms = 0.02
epsilon = 1e-06
smallest_normal = 0.015625

step_unit = 1024.0


def exchanged(blocks, axis):
    return lax.all_to_all(blocks, axis, split_axis=0, concat_axis=0, tiled=True)


def to_everyone(value, axis):
    copies = jnp.broadcast_to(value, (lax.axis_size(axis), *value.shape))
    return exchanged(copies, axis)


def smallest_scale(peaks):
    target = peaks * (1.0 / code_limit)
    spread = target * (2.0**23 + 1.0)
    scale = spread - (spread - target)
    scale = jnp.where(code_limit * scale < peaks, 2.0 * scale, scale)
    return jnp.where(code_limit * (0.5 * scale) >= peaks, 0.5 * scale, scale)


def encode_kernel(base_ref, inner_ref, decoded_ref):
    for at in range(0, base_ref.shape[1], BLOCK):
        columns = pl.ds(at, BLOCK)
        deltas = base_ref[:, columns] - inner_ref[:, columns].astype(jnp.float32)
        magnitude = jnp.abs(deltas)
        scale = smallest_scale(jnp.max(magnitude, axis=1, keepdims=True) + epsilon)
        beyond = deltas * (1.0 + 2.0**-23)
        spread = beyond * (2.0**20 + 1.0)
        normal = spread - (spread - beyond)
        anchor = scale * (1.5 * 2.0**14)
        small = (beyond + anchor) - anchor
        decoded = jnp.where(magnitude < scale * smallest_normal, small, normal)
        decoded_ref[:, columns] = decoded.astype(decoded_ref.dtype)


def decoded_deltas(base_weights, replica_copy):
    rows, columns = base_weights.shape
    tall = rows // 2
    spec = pl.BlockSpec((tall, columns), lambda i: (i, 0))
    return pl.pallas_call(
        encode_kernel,
        grid=(rows // tall,),
        in_specs=[spec, spec],
        out_specs=spec,
        out_shape=jax.ShapeDtypeStruct((rows, columns), jnp.bfloat16),
        cost_estimate=pl.CostEstimate(
            flops=20 * rows * columns, bytes_accessed=8 * rows * columns, transcendentals=0
        ),
    )(base_weights, replica_copy)


def lane_squares(value):
    rows, columns = value.shape
    tiles = (value * value).reshape(rows // 8, 8, columns // 128, 128)
    return tiles.sum(axis=(0, 1, 2))[None]


def lane_total(lanes, columns):
    ones = jnp.ones((lanes.shape[1], columns), lanes.dtype)
    return lax.dot(lanes, ones, precision=lax.Precision.HIGHEST)


def shards(base_weights, inner_weights, momentum):
    replicas = lax.axis_size(REPLICA)
    local_rows, columns = base_weights.shape
    owned_rows = local_rows // replicas
    replica_copy = inner_weights[0]
    decoded = decoded_deltas(base_weights, replica_copy)
    arrived = exchanged(decoded.reshape(replicas, owned_rows, columns), REPLICA)
    blended = blend_share * replica_copy.astype(jnp.float32) + (1.0 - blend_share) * base_weights
    kept = outer_momentum * momentum
    arrived, blended, kept = lax.optimization_barrier((arrived, blended, kept))
    outer_grad = arrived.astype(jnp.float32).sum(axis=0) / replicas
    squares = to_everyone(lane_squares(outer_grad), RING).sum(axis=0)
    squares = to_everyone(squares, PLANE).sum(axis=0)
    grad_sq = lane_total(squares, columns)
    clip_factor = jnp.minimum(1.0, clip_rms / jnp.sqrt(grad_sq / (D * KVW) + epsilon))
    step_term = clip_factor * outer_grad
    new_momentum = kept + step_term
    step = outer_rate * (step_term + outer_momentum * new_momentum)
    steps = to_everyone((step * step_unit).astype(jnp.float16), REPLICA)
    steps = lax.optimization_barrier(steps.reshape(local_rows, columns))
    steps = steps.astype(jnp.float32) * (1.0 / step_unit)
    new_inner = (blended - (1.0 - blend_share) * steps).astype(jnp.bfloat16)
    return (base_weights - steps, new_momentum, new_inner[None])


def solution(mesh):
    torus = Mesh(
        mesh.devices.reshape(4, 4, 8, 2, 2),
        ("replica_0", "replica_1", "fsdp_0", "fsdp_1", "fsdp_2"),
    )
    return jax.shard_map(
        shards,
        mesh=torus,
        in_specs=(P(FSDP, None), P(REPLICA, FSDP, None), P(FSDP_REPLICA, None)),
        out_specs=(P(FSDP, None), P(FSDP_REPLICA, None), P(REPLICA, FSDP, None)),
        check_vma=False,
    )
```

```python
import jax
import jax.numpy as jnp
from jax import lax
from jax.experimental import pallas as pl
from jax.experimental.pallas import tpu as pltpu
from jax.sharding import Mesh
from jax.sharding import PartitionSpec as P

D = 8192
KVW = 1024
BLOCK = 128
REPLICA = ("replica_0", "replica_1")
FSDP = ("fsdp_0", "fsdp_1", "fsdp_2")
FSDP_REPLICA = ("fsdp_0", "fsdp_1", "fsdp_2", "replica_0", "replica_1")
RING = ("fsdp_1", "replica_0", "fsdp_2")
PLANE = ("replica_1", "fsdp_0")

code_limit = 448.0
outer_rate = 0.7
outer_momentum = 0.9
blend_share = 0.5
clip_rms = 0.02
epsilon = 1e-06
smallest_normal = 0.015625

step_unit = 1024.0


def exchanged(blocks, axis):
    return lax.all_to_all(blocks, axis, split_axis=0, concat_axis=0, tiled=True)


def to_everyone(value, axis):
    copies = jnp.broadcast_to(value, (lax.axis_size(axis), *value.shape))
    return exchanged(copies, axis)


def smallest_scale(peaks):
    target = peaks * (1.0 / code_limit)
    spread = target * (2.0**23 + 1.0)
    scale = spread - (spread - target)
    scale = jnp.where(code_limit * scale < peaks, 2.0 * scale, scale)
    return jnp.where(code_limit * (0.5 * scale) >= peaks, 0.5 * scale, scale)


def encode_kernel(base_ref, inner_ref, decoded_ref):
    for at in range(0, base_ref.shape[1], BLOCK):
        columns = pl.ds(at, BLOCK)
        deltas = base_ref[:, columns] - inner_ref[:, columns].astype(jnp.float32)
        magnitude = jnp.abs(deltas)
        scale = smallest_scale(jnp.max(magnitude, axis=1, keepdims=True) + epsilon)
        beyond = deltas * (1.0 + 2.0**-23)
        spread = beyond * (2.0**20 + 1.0)
        normal = spread - (spread - beyond)
        anchor = scale * (1.5 * 2.0**14)
        small = (beyond + anchor) - anchor
        decoded = jnp.where(magnitude < scale * smallest_normal, small, normal)
        decoded_ref[:, columns] = decoded.astype(decoded_ref.dtype)


def decoded_deltas(base_weights, replica_copy):
    rows, columns = base_weights.shape
    tall = rows // 2
    spec = pl.BlockSpec((tall, columns), lambda i: (i, 0))
    return pl.pallas_call(
        encode_kernel,
        grid=(rows // tall,),
        in_specs=[spec, spec],
        out_specs=spec,
        out_shape=jax.ShapeDtypeStruct((rows, columns), jnp.bfloat16),
        cost_estimate=pl.CostEstimate(
            flops=20 * rows * columns, bytes_accessed=8 * rows * columns, transcendentals=0
        ),
    )(base_weights, replica_copy)


def outputs_kernel(chunk, base_ref, blended_ref, steps_ref, kept_ref, grad_ref, clip_ref, *refs):
    out_refs, held_refs, sems = refs[:3], refs[3:6], refs[6]
    base_held, momentum_held, inner_held = held_refs

    def copy(which, part, rows):
        return pltpu.make_async_copy(
            held_refs[which].at[rows], out_refs[which].at[rows], sems.at[which, part]
        )

    copies = []
    momentum_held[...] = kept_ref[...] + clip_ref[...] * grad_ref[...]
    copies.append(copy(1, 0, pl.ds(0, momentum_held.shape[0])))
    copies[-1].start()
    for part in range(base_held.shape[0] // chunk):
        rows = pl.ds(part * chunk, chunk)
        steps = steps_ref[rows]
        base_held[rows] = base_ref[rows] - steps
        copies.append(copy(0, part, rows))
        copies[-1].start()
        inner_held[rows] = (blended_ref[rows] - (1.0 - blend_share) * steps).astype(jnp.bfloat16)
        copies.append(copy(2, part, rows))
        copies[-1].start()
    for each in copies:
        each.wait()


def outputs(base_weights, blended, steps, kept, outer_grad, clip_factor):
    rows, columns = base_weights.shape
    chunk = rows // 4
    shapes = (
        jax.ShapeDtypeStruct((rows, columns), jnp.float32),
        jax.ShapeDtypeStruct(kept.shape, jnp.float32),
        jax.ShapeDtypeStruct((rows, columns), jnp.bfloat16),
    )
    return pl.pallas_call(
        lambda *refs: outputs_kernel(chunk, *refs),
        in_specs=[pl.BlockSpec(memory_space=pltpu.VMEM)] * 6,
        out_specs=[pl.BlockSpec(memory_space=pl.ANY)] * 3,
        out_shape=shapes,
        scratch_shapes=[pltpu.VMEM(each.shape, each.dtype) for each in shapes]
        + [pltpu.SemaphoreType.DMA((3, 4))],
        compiler_params=pltpu.CompilerParams(vmem_limit_bytes=8 * 2**20),
        cost_estimate=pl.CostEstimate(
            flops=4 * rows * columns, bytes_accessed=18 * rows * columns, transcendentals=0
        ),
    )(base_weights, blended, steps, kept, outer_grad, clip_factor)


def lane_squares(value):
    rows, columns = value.shape
    tiles = (value * value).reshape(rows // 8, 8, columns // 128, 128)
    return tiles.sum(axis=(0, 1, 2))[None]


def lane_total(lanes, columns):
    ones = jnp.ones((lanes.shape[1], columns), lanes.dtype)
    return lax.dot(lanes, ones, precision=lax.Precision.HIGHEST)


def shards(base_weights, inner_weights, momentum):
    replicas = lax.axis_size(REPLICA)
    local_rows, columns = base_weights.shape
    owned_rows = local_rows // replicas
    replica_copy = inner_weights[0]
    decoded = decoded_deltas(base_weights, replica_copy)
    arrived = exchanged(decoded.reshape(replicas, owned_rows, columns), REPLICA)
    blended = blend_share * replica_copy.astype(jnp.float32) + (1.0 - blend_share) * base_weights
    kept = outer_momentum * momentum
    arrived, blended, kept = lax.optimization_barrier((arrived, blended, kept))
    outer_grad = arrived.astype(jnp.float32).sum(axis=0) / replicas
    squares = to_everyone(lane_squares(outer_grad), RING).sum(axis=0)
    squares = to_everyone(squares, PLANE).sum(axis=0)
    grad_sq = lane_total(squares, columns)
    clip_factor = jnp.minimum(1.0, clip_rms / jnp.sqrt(grad_sq / (D * KVW) + epsilon))
    step_term = clip_factor * outer_grad
    step = outer_rate * (step_term + outer_momentum * (kept + step_term))
    steps = to_everyone((step * step_unit).astype(jnp.float16), REPLICA)
    steps = steps.reshape(local_rows, columns).astype(jnp.float32) * (1.0 / step_unit)
    new_base, new_momentum, new_inner = outputs(
        base_weights, blended, steps, kept, outer_grad, clip_factor
    )
    return (new_base, new_momentum, new_inner[None])


def solution(mesh):
    torus = Mesh(
        mesh.devices.reshape(4, 4, 8, 2, 2),
        ("replica_0", "replica_1", "fsdp_0", "fsdp_1", "fsdp_2"),
    )
    return jax.shard_map(
        shards,
        mesh=torus,
        in_specs=(P(FSDP, None), P(REPLICA, FSDP, None), P(FSDP_REPLICA, None)),
        out_specs=(P(FSDP, None), P(FSDP_REPLICA, None), P(REPLICA, FSDP, None)),
        check_vma=False,
    )
```

```python
import jax
import jax.numpy as jnp
from jax import lax
from jax.experimental import pallas as pl
from jax.experimental.pallas import tpu as pltpu
from jax.sharding import Mesh
from jax.sharding import PartitionSpec as P

D = 8192
KVW = 1024
BLOCK = 128
REPLICA = ("replica_0", "replica_1")
FSDP = ("fsdp_0", "fsdp_1", "fsdp_2")
FSDP_REPLICA = ("fsdp_0", "fsdp_1", "fsdp_2", "replica_0", "replica_1")
RING = ("fsdp_1", "replica_0", "fsdp_2")
PLANE = ("replica_1", "fsdp_0")

code_limit = 448.0
outer_rate = 0.7
outer_momentum = 0.9
blend_share = 0.5
clip_rms = 0.02
epsilon = 1e-06
smallest_normal = 0.015625

step_unit = 1024.0


def exchanged(blocks, axis):
    return lax.all_to_all(blocks, axis, split_axis=0, concat_axis=0, tiled=True)


def to_everyone(value, axis):
    copies = jnp.broadcast_to(value, (lax.axis_size(axis), *value.shape))
    return exchanged(copies, axis)


def smallest_scale(peaks):
    spread = peaks * (2.0**23 + 1.0)
    near = spread - (spread - peaks)
    return jnp.where(peaks <= (code_limit / 512.0) * near, 0.5 * near, near)


def encoded(base_block, inner_block):
    deltas = base_block - inner_block.astype(jnp.float32)
    magnitude = jnp.abs(deltas)
    scale = smallest_scale(jnp.max(magnitude, axis=1, keepdims=True) + epsilon)
    beyond = deltas * (1.0 + 2.0**-23)
    spread = beyond * (2.0**20 + 1.0)
    normal = spread - (spread - beyond)
    anchor = scale * (1.5 * 2.0**6)
    small = (beyond + anchor) - anchor
    return jnp.where(magnitude < scale * (smallest_normal / 256.0), small, normal)


def encode_kernel(chunk, base_hbm, inner_hbm, decoded_ref, base_ref, inner_ref, sems):
    parts = range(base_ref.shape[0] // chunk)

    def arriving(part):
        rows = pl.ds(part * chunk, chunk)
        return [
            pltpu.make_async_copy(source.at[rows], target.at[rows], sems.at[which, part])
            for which, (source, target) in enumerate(
                [(base_hbm, base_ref), (inner_hbm, inner_ref)]
            )
        ]

    for part in parts:
        for each in arriving(part):
            each.start()
    for part in parts:
        for each in arriving(part):
            each.wait()
        rows = pl.ds(part * chunk, chunk)
        for at in range(0, base_ref.shape[1], BLOCK):
            lanes = pl.ds(at, BLOCK)
            decoded = encoded(base_ref[rows, lanes], inner_ref[rows, lanes])
            decoded_ref[rows, lanes] = decoded.astype(decoded_ref.dtype)


def decoded_deltas(base_weights, replica_copy):
    rows, columns = base_weights.shape
    chunk = rows // 4
    return pl.pallas_call(
        lambda *refs: encode_kernel(chunk, *refs),
        in_specs=[pl.BlockSpec(memory_space=pltpu.HBM)] * 2,
        out_specs=[pl.BlockSpec(memory_space=pltpu.VMEM)] * 3,
        out_shape=[
            jax.ShapeDtypeStruct((rows, columns), jnp.bfloat16),
            jax.ShapeDtypeStruct((rows, columns), jnp.float32),
            jax.ShapeDtypeStruct((rows, columns), jnp.bfloat16),
        ],
        scratch_shapes=[pltpu.SemaphoreType.DMA((2, 4))],
        compiler_params=pltpu.CompilerParams(vmem_limit_bytes=51 * 2**20),
        cost_estimate=pl.CostEstimate(
            flops=20 * rows * columns, bytes_accessed=8 * rows * columns, transcendentals=0
        ),
    )(base_weights, replica_copy)


def outputs_kernel(chunk, base_ref, inner_ref, steps_ref, kept_ref, grad_ref, clip_ref, *refs):
    out_refs, held_refs, sems = refs[:3], refs[3:6], refs[6]
    base_held, momentum_held, inner_held = held_refs

    def copy(which, part, rows):
        return pltpu.make_async_copy(
            held_refs[which].at[rows], out_refs[which].at[rows], sems.at[which, part]
        )

    copies = []
    momentum_held[...] = kept_ref[...] + clip_ref[...] * grad_ref[...]
    copies.append(copy(1, 0, pl.ds(0, momentum_held.shape[0])))
    copies[-1].start()
    for part in range(base_held.shape[0] // chunk):
        rows = pl.ds(part * chunk, chunk)
        new_base = base_ref[rows] - steps_ref[rows]
        base_held[rows] = new_base
        copies.append(copy(0, part, rows))
        copies[-1].start()
        kept_share = blend_share * inner_ref[rows].astype(jnp.float32)
        inner_held[rows] = (kept_share + (1.0 - blend_share) * new_base).astype(jnp.bfloat16)
        copies.append(copy(2, part, rows))
        copies[-1].start()
    for each in copies:
        each.wait()


def outputs(base_weights, replica_copy, steps, kept, outer_grad, clip_factor):
    rows, columns = base_weights.shape
    chunk = rows // 4
    shapes = (
        jax.ShapeDtypeStruct((rows, columns), jnp.float32),
        jax.ShapeDtypeStruct(kept.shape, jnp.float32),
        jax.ShapeDtypeStruct((rows, columns), jnp.bfloat16),
    )
    return pl.pallas_call(
        lambda *refs: outputs_kernel(chunk, *refs),
        in_specs=[pl.BlockSpec(memory_space=pltpu.VMEM)] * 6,
        out_specs=[pl.BlockSpec(memory_space=pl.ANY)] * 3,
        out_shape=shapes,
        scratch_shapes=[pltpu.VMEM(each.shape, each.dtype) for each in shapes]
        + [pltpu.SemaphoreType.DMA((3, 4))],
        compiler_params=pltpu.CompilerParams(vmem_limit_bytes=8 * 2**20),
        cost_estimate=pl.CostEstimate(
            flops=4 * rows * columns, bytes_accessed=18 * rows * columns, transcendentals=0
        ),
    )(base_weights, replica_copy, steps, kept, outer_grad, clip_factor)


def lane_squares(value):
    rows, columns = value.shape
    tiles = (value * value).reshape(rows // 8, 8, columns // 128, 128)
    return tiles.sum(axis=(0, 1, 2))[None]


def lane_total(lanes, columns):
    ones = jnp.ones((lanes.shape[1], columns), lanes.dtype)
    return lax.dot(lanes, ones, precision=lax.Precision.HIGHEST)


def shards(base_weights, inner_weights, momentum):
    replicas = lax.axis_size(REPLICA)
    local_rows, columns = base_weights.shape
    owned_rows = local_rows // replicas
    decoded, base_weights, replica_copy = decoded_deltas(base_weights, inner_weights[0])
    arrived = exchanged(decoded.reshape(replicas, owned_rows, columns), REPLICA)
    arrived, momentum = lax.optimization_barrier((arrived, momentum))
    kept = outer_momentum * momentum
    outer_grad = arrived.astype(jnp.float32).sum(axis=0) / replicas
    squares = to_everyone(lane_squares(outer_grad), RING).sum(axis=0)
    squares = to_everyone(squares, PLANE).sum(axis=0)
    grad_sq = lane_total(squares, columns)
    clip_factor = jnp.minimum(1.0, clip_rms / jnp.sqrt(grad_sq / (D * KVW) + epsilon))
    step_term = clip_factor * outer_grad
    step = outer_rate * (step_term + outer_momentum * (kept + step_term))
    steps = to_everyone((step * step_unit).astype(jnp.float16), REPLICA)
    steps = steps.reshape(local_rows, columns).astype(jnp.float32) * (1.0 / step_unit)
    new_base, new_momentum, new_inner = outputs(
        base_weights, replica_copy, steps, kept, outer_grad, clip_factor
    )
    return (new_base, new_momentum, new_inner[None])


def solution(mesh):
    torus = Mesh(
        mesh.devices.reshape(4, 4, 8, 2, 2),
        ("replica_0", "replica_1", "fsdp_0", "fsdp_1", "fsdp_2"),
    )
    return jax.shard_map(
        shards,
        mesh=torus,
        in_specs=(P(FSDP, None), P(REPLICA, FSDP, None), P(FSDP_REPLICA, None)),
        out_specs=(P(FSDP, None), P(FSDP_REPLICA, None), P(REPLICA, FSDP, None)),
        check_vma=False,
    )
```

```python
import jax
import jax.numpy as jnp
from jax import lax
from jax.experimental import pallas as pl
from jax.experimental.pallas import tpu as pltpu
from jax.sharding import Mesh
from jax.sharding import PartitionSpec as P

D = 8192
KVW = 1024
BLOCK = 128
REPLICA = ("replica_0", "replica_1")
FSDP = ("fsdp_0", "fsdp_1", "fsdp_2")
FSDP_REPLICA = ("fsdp_0", "fsdp_1", "fsdp_2", "replica_0", "replica_1")
RING = ("fsdp_1", "replica_0", "fsdp_2")
PLANE = ("replica_1", "fsdp_0")

code_limit = 448.0
outer_rate = 0.7
outer_momentum = 0.9
blend_share = 0.5
clip_rms = 0.02
epsilon = 1e-06
smallest_normal = 0.015625

step_unit = 1024.0


def exchanged(blocks, axis):
    return lax.all_to_all(blocks, axis, split_axis=0, concat_axis=0, tiled=True)


def to_everyone(value, axis):
    copies = jnp.broadcast_to(value, (lax.axis_size(axis), *value.shape))
    return exchanged(copies, axis)


def smallest_scale(peaks):
    spread = peaks * (2.0**23 + 1.0)
    near = spread - (spread - peaks)
    return jnp.where(peaks <= (code_limit / 512.0) * near, 0.5 * near, near)


def encoded(base_block, inner_block):
    deltas = base_block - inner_block.astype(jnp.float32)
    magnitude = jnp.abs(deltas)
    scale = smallest_scale(jnp.max(magnitude, axis=1, keepdims=True) + epsilon)
    beyond = deltas * (1.0 + 2.0**-23)
    spread = beyond * (2.0**20 + 1.0)
    normal = spread - (spread - beyond)
    anchor = scale * (1.5 * 2.0**6)
    small = (beyond + anchor) - anchor
    return jnp.where(magnitude < scale * (smallest_normal / 256.0), small, normal)


def encode_kernel(chunk, base_hbm, inner_hbm, decoded_ref, base_ref, inner_ref, sems):
    parts = range(base_ref.shape[0] // chunk)

    def arriving(part):
        rows = pl.ds(part * chunk, chunk)
        return [
            pltpu.make_async_copy(source.at[rows], target.at[rows], sems.at[which, part])
            for which, (source, target) in enumerate(
                [(base_hbm, base_ref), (inner_hbm, inner_ref)]
            )
        ]

    for part in parts:
        for each in arriving(part):
            each.start()
    for part in parts:
        for each in arriving(part):
            each.wait()
        rows = pl.ds(part * chunk, chunk)
        for at in range(0, base_ref.shape[1], BLOCK):
            lanes = pl.ds(at, BLOCK)
            decoded = encoded(base_ref[rows, lanes], inner_ref[rows, lanes])
            decoded_ref[rows, lanes] = decoded.astype(decoded_ref.dtype)


def decoded_deltas(base_weights, replica_copy):
    rows, columns = base_weights.shape
    chunk = rows // 4
    return pl.pallas_call(
        lambda *refs: encode_kernel(chunk, *refs),
        in_specs=[pl.BlockSpec(memory_space=pltpu.HBM)] * 2,
        out_specs=pl.BlockSpec(memory_space=pltpu.VMEM),
        out_shape=jax.ShapeDtypeStruct((rows, columns), jnp.bfloat16),
        scratch_shapes=[
            pltpu.VMEM((rows, columns), jnp.float32),
            pltpu.VMEM((rows, columns), jnp.bfloat16),
            pltpu.SemaphoreType.DMA((2, 4)),
        ],
        compiler_params=pltpu.CompilerParams(vmem_limit_bytes=53 * 2**20),
        cost_estimate=pl.CostEstimate(
            flops=20 * rows * columns, bytes_accessed=8 * rows * columns, transcendentals=0
        ),
    )(base_weights, replica_copy)


def outputs_kernel(chunk, base_ref, blended_ref, steps_ref, kept_ref, grad_ref, clip_ref, *refs):
    out_refs, held_refs, sems = refs[:3], refs[3:6], refs[6]
    base_held, momentum_held, inner_held = held_refs

    def copy(which, part, rows):
        return pltpu.make_async_copy(
            held_refs[which].at[rows], out_refs[which].at[rows], sems.at[which, part]
        )

    copies = []
    momentum_held[...] = kept_ref[...] + clip_ref[...] * grad_ref[...]
    copies.append(copy(1, 0, pl.ds(0, momentum_held.shape[0])))
    copies[-1].start()
    for part in range(base_held.shape[0] // chunk):
        rows = pl.ds(part * chunk, chunk)
        steps = steps_ref[rows]
        base_held[rows] = base_ref[rows] - steps
        copies.append(copy(0, part, rows))
        copies[-1].start()
        inner_held[rows] = (blended_ref[rows] - (1.0 - blend_share) * steps).astype(jnp.bfloat16)
        copies.append(copy(2, part, rows))
        copies[-1].start()
    for each in copies:
        each.wait()


def outputs(base_weights, blended, steps, kept, outer_grad, clip_factor):
    rows, columns = base_weights.shape
    chunk = rows // 4
    shapes = (
        jax.ShapeDtypeStruct((rows, columns), jnp.float32),
        jax.ShapeDtypeStruct(kept.shape, jnp.float32),
        jax.ShapeDtypeStruct((rows, columns), jnp.bfloat16),
    )
    return pl.pallas_call(
        lambda *refs: outputs_kernel(chunk, *refs),
        in_specs=[pl.BlockSpec(memory_space=pltpu.VMEM)] * 6,
        out_specs=[pl.BlockSpec(memory_space=pl.ANY)] * 3,
        out_shape=shapes,
        scratch_shapes=[pltpu.VMEM(each.shape, each.dtype) for each in shapes]
        + [pltpu.SemaphoreType.DMA((3, 4))],
        compiler_params=pltpu.CompilerParams(vmem_limit_bytes=8 * 2**20),
        cost_estimate=pl.CostEstimate(
            flops=4 * rows * columns, bytes_accessed=18 * rows * columns, transcendentals=0
        ),
    )(base_weights, blended, steps, kept, outer_grad, clip_factor)


def lane_squares(value):
    rows, columns = value.shape
    tiles = (value * value).reshape(rows // 8, 8, columns // 128, 128)
    return tiles.sum(axis=(0, 1, 2))[None]


def lane_total(lanes, columns):
    ones = jnp.ones((lanes.shape[1], columns), lanes.dtype)
    return lax.dot(lanes, ones, precision=lax.Precision.HIGHEST)


def shards(base_weights, inner_weights, momentum):
    replicas = lax.axis_size(REPLICA)
    local_rows, columns = base_weights.shape
    owned_rows = local_rows // replicas
    decoded = decoded_deltas(base_weights, inner_weights[0])
    arrived = exchanged(decoded.reshape(replicas, owned_rows, columns), REPLICA)
    outer_grad = arrived.astype(jnp.float32).sum(axis=0) / replicas
    squares = to_everyone(lane_squares(outer_grad), RING).sum(axis=0)
    squares, base_weights, inner_weights, momentum = lax.optimization_barrier(
        (squares, base_weights, inner_weights, momentum)
    )
    replica_copy = inner_weights[0].astype(jnp.float32)
    blended = blend_share * replica_copy + (1.0 - blend_share) * base_weights
    squares, blended, kept = lax.optimization_barrier(
        (squares, blended, outer_momentum * momentum)
    )
    squares = to_everyone(squares, PLANE).sum(axis=0)
    grad_sq = lane_total(squares, columns)
    clip_factor = jnp.minimum(1.0, clip_rms / jnp.sqrt(grad_sq / (D * KVW) + epsilon))
    step_term = clip_factor * outer_grad
    step = outer_rate * (step_term + outer_momentum * (kept + step_term))
    steps = to_everyone((step * step_unit).astype(jnp.float16), REPLICA)
    steps = steps.reshape(local_rows, columns).astype(jnp.float32) * (1.0 / step_unit)
    new_base, new_momentum, new_inner = outputs(
        base_weights, blended, steps, kept, outer_grad, clip_factor
    )
    return (new_base, new_momentum, new_inner[None])


def solution(mesh):
    torus = Mesh(
        mesh.devices.reshape(4, 4, 8, 2, 2),
        ("replica_0", "replica_1", "fsdp_0", "fsdp_1", "fsdp_2"),
    )
    return jax.shard_map(
        shards,
        mesh=torus,
        in_specs=(P(FSDP, None), P(REPLICA, FSDP, None), P(FSDP_REPLICA, None)),
        out_specs=(P(FSDP, None), P(FSDP_REPLICA, None), P(REPLICA, FSDP, None)),
        check_vma=False,
    )
```

```python
import jax
import jax.numpy as jnp
from jax import lax
from jax.experimental import pallas as pl
from jax.experimental.pallas import tpu as pltpu
from jax.sharding import Mesh
from jax.sharding import PartitionSpec as P

D = 8192
KVW = 1024
BLOCK = 128
REPLICA = ("replica_0", "replica_1")
FSDP = ("fsdp_0", "fsdp_1", "fsdp_2")
FSDP_REPLICA = ("fsdp_0", "fsdp_1", "fsdp_2", "replica_0", "replica_1")
RING = ("fsdp_1", "replica_0", "fsdp_2")
PLANE = ("replica_1", "fsdp_0")

code_limit = 448.0
outer_rate = 0.7
outer_momentum = 0.9
blend_share = 0.5
clip_rms = 0.02
epsilon = 1e-06
smallest_normal = 0.015625

step_unit = 1024.0


def exchanged(blocks, axis):
    return lax.all_to_all(blocks, axis, split_axis=0, concat_axis=0, tiled=True)


def to_everyone(value, axis):
    copies = jnp.broadcast_to(value, (lax.axis_size(axis), *value.shape))
    return exchanged(copies, axis)


def smallest_scale(peaks):
    spread = peaks * (2.0**23 + 1.0)
    near = spread - (spread - peaks)
    return jnp.where(peaks <= (code_limit / 512.0) * near, 0.5 * near, near)


def encoded(base_block, inner_block):
    deltas = base_block - inner_block.astype(jnp.float32)
    magnitude = jnp.abs(deltas)
    scale = smallest_scale(jnp.max(magnitude, axis=1, keepdims=True) + epsilon)
    beyond = deltas * (1.0 + 2.0**-23)
    spread = beyond * (2.0**20 + 1.0)
    normal = spread - (spread - beyond)
    anchor = scale * (1.5 * 2.0**6)
    small = (beyond + anchor) - anchor
    return jnp.where(magnitude < scale * (smallest_normal / 256.0), small, normal)


def encode_kernel(chunk, base_hbm, inner_hbm, decoded_ref, base_ref, inner_ref, sems):
    parts = range(base_ref.shape[0] // chunk)

    def arriving(part):
        rows = pl.ds(part * chunk, chunk)
        return [
            pltpu.make_async_copy(source.at[rows], target.at[rows], sems.at[which, part])
            for which, (source, target) in enumerate(
                [(base_hbm, base_ref), (inner_hbm, inner_ref)]
            )
        ]

    for part in parts:
        for each in arriving(part):
            each.start()
    for part in parts:
        for each in arriving(part):
            each.wait()
        rows = pl.ds(part * chunk, chunk)
        for at in range(0, base_ref.shape[1], BLOCK):
            lanes = pl.ds(at, BLOCK)
            decoded = encoded(base_ref[rows, lanes], inner_ref[rows, lanes])
            decoded_ref[rows, lanes] = decoded.astype(decoded_ref.dtype)


def decoded_deltas(base_weights, replica_copy):
    rows, columns = base_weights.shape
    chunk = rows // 4
    return pl.pallas_call(
        lambda *refs: encode_kernel(chunk, *refs),
        in_specs=[pl.BlockSpec(memory_space=pltpu.HBM)] * 2,
        out_specs=pl.BlockSpec(memory_space=pltpu.VMEM),
        out_shape=jax.ShapeDtypeStruct((rows, columns), jnp.bfloat16),
        scratch_shapes=[
            pltpu.VMEM((rows, columns), jnp.float32),
            pltpu.VMEM((rows, columns), jnp.bfloat16),
            pltpu.SemaphoreType.DMA((2, 4)),
        ],
        compiler_params=pltpu.CompilerParams(vmem_limit_bytes=53 * 2**20),
        cost_estimate=pl.CostEstimate(
            flops=20 * rows * columns, bytes_accessed=8 * rows * columns, transcendentals=0
        ),
    )(base_weights, replica_copy)


def outputs_kernel(chunk, base_ref, blended_ref, steps_ref, kept_ref, grad_ref, clip_ref, *refs):
    out_refs, held_refs, sems = refs[:3], refs[3:6], refs[6]
    base_held, momentum_held, inner_held = held_refs

    def copy(which, part, rows):
        return pltpu.make_async_copy(
            held_refs[which].at[rows], out_refs[which].at[rows], sems.at[which, part]
        )

    copies = []
    momentum_held[...] = kept_ref[...] + clip_ref[...] * grad_ref[...]
    copies.append(copy(1, 0, pl.ds(0, momentum_held.shape[0])))
    copies[-1].start()
    for part in range(base_held.shape[0] // chunk):
        rows = pl.ds(part * chunk, chunk)
        steps = steps_ref[rows]
        base_held[rows] = base_ref[rows] - steps
        copies.append(copy(0, part, rows))
        copies[-1].start()
        inner_held[rows] = (blended_ref[rows] - (1.0 - blend_share) * steps).astype(jnp.bfloat16)
        copies.append(copy(2, part, rows))
        copies[-1].start()
    for each in copies:
        each.wait()


def outputs(base_weights, blended, steps, kept, outer_grad, clip_factor):
    rows, columns = base_weights.shape
    chunk = rows // 2
    shapes = (
        jax.ShapeDtypeStruct((rows, columns), jnp.float32),
        jax.ShapeDtypeStruct(kept.shape, jnp.float32),
        jax.ShapeDtypeStruct((rows, columns), jnp.bfloat16),
    )
    return pl.pallas_call(
        lambda *refs: outputs_kernel(chunk, *refs),
        in_specs=[pl.BlockSpec(memory_space=pltpu.VMEM)] * 6,
        out_specs=[pl.BlockSpec(memory_space=pl.ANY)] * 3,
        out_shape=shapes,
        scratch_shapes=[pltpu.VMEM(each.shape, each.dtype) for each in shapes]
        + [pltpu.SemaphoreType.DMA((3, 2))],
        compiler_params=pltpu.CompilerParams(vmem_limit_bytes=8 * 2**20),
        cost_estimate=pl.CostEstimate(
            flops=4 * rows * columns, bytes_accessed=18 * rows * columns, transcendentals=0
        ),
    )(base_weights, blended, steps, kept, outer_grad, clip_factor)


def lane_squares(value):
    rows, columns = value.shape
    tiles = (value * value).reshape(rows // 8, 8, columns // 128, 128)
    return tiles.sum(axis=(0, 1, 2))[None]


def lane_total(lanes, columns):
    ones = jnp.ones((lanes.shape[1], columns), lanes.dtype)
    return lax.dot(lanes, ones, precision=lax.Precision.HIGHEST)


def shards(base_weights, inner_weights, momentum):
    replicas = lax.axis_size(REPLICA)
    local_rows, columns = base_weights.shape
    owned_rows = local_rows // replicas
    decoded = decoded_deltas(base_weights, inner_weights[0])
    arrived = exchanged(decoded.reshape(replicas, owned_rows, columns), REPLICA)
    outer_grad = arrived.astype(jnp.float32).sum(axis=0) / replicas
    squares = to_everyone(lane_squares(outer_grad), RING).sum(axis=0)
    squares, base_weights, inner_weights, momentum = lax.optimization_barrier(
        (squares, base_weights, inner_weights, momentum)
    )
    replica_copy = inner_weights[0].astype(jnp.float32)
    blended = blend_share * replica_copy + (1.0 - blend_share) * base_weights
    squares, blended, kept = lax.optimization_barrier(
        (squares, blended, outer_momentum * momentum)
    )
    squares = to_everyone(squares, PLANE).sum(axis=0)
    grad_sq = lane_total(squares, columns)
    clip_factor = jnp.minimum(1.0, clip_rms / jnp.sqrt(grad_sq / (D * KVW) + epsilon))
    step_term = clip_factor * outer_grad
    step = outer_rate * (step_term + outer_momentum * (kept + step_term))
    steps = to_everyone((step * step_unit).astype(jnp.float16), REPLICA)
    steps = steps.reshape(local_rows, columns).astype(jnp.float32) * (1.0 / step_unit)
    new_base, new_momentum, new_inner = outputs(
        base_weights, blended, steps, kept, outer_grad, clip_factor
    )
    return (new_base, new_momentum, new_inner[None])


def solution(mesh):
    torus = Mesh(
        mesh.devices.reshape(4, 4, 8, 2, 2),
        ("replica_0", "replica_1", "fsdp_0", "fsdp_1", "fsdp_2"),
    )
    return jax.shard_map(
        shards,
        mesh=torus,
        in_specs=(P(FSDP, None), P(REPLICA, FSDP, None), P(FSDP_REPLICA, None)),
        out_specs=(P(FSDP, None), P(FSDP_REPLICA, None), P(REPLICA, FSDP, None)),
        check_vma=False,
    )
```

```python
import jax
import jax.numpy as jnp
from jax import lax
from jax.experimental import pallas as pl
from jax.experimental.pallas import tpu as pltpu
from jax.sharding import Mesh
from jax.sharding import PartitionSpec as P

D = 8192
KVW = 1024
BLOCK = 128
REPLICA = ("replica_0", "replica_1")
FSDP = ("fsdp_0", "fsdp_1", "fsdp_2")
FSDP_REPLICA = ("fsdp_0", "fsdp_1", "fsdp_2", "replica_0", "replica_1")
RING = ("fsdp_0", "fsdp_2")
PLANE = ("replica_1", "fsdp_1", "replica_0")

code_limit = 448.0
outer_rate = 0.7
outer_momentum = 0.9
blend_share = 0.5
clip_rms = 0.02
epsilon = 1e-06
smallest_normal = 0.015625

step_unit = 1024.0


def exchanged(blocks, axis):
    return lax.all_to_all(blocks, axis, split_axis=0, concat_axis=0, tiled=True)


def to_everyone(value, axis):
    copies = jnp.broadcast_to(value, (lax.axis_size(axis), *value.shape))
    return exchanged(copies, axis)


def smallest_scale(peaks):
    spread = peaks * (2.0**23 + 1.0)
    near = spread - (spread - peaks)
    return jnp.where(peaks <= (code_limit / 512.0) * near, 0.5 * near, near)


def encoded(base_block, inner_block):
    deltas = base_block - inner_block.astype(jnp.float32)
    magnitude = jnp.abs(deltas)
    scale = smallest_scale(jnp.max(magnitude, axis=1, keepdims=True) + epsilon)
    beyond = deltas * (1.0 + 2.0**-23)
    spread = beyond * (2.0**20 + 1.0)
    normal = spread - (spread - beyond)
    anchor = scale * (1.5 * 2.0**6)
    small = (beyond + anchor) - anchor
    return jnp.where(magnitude < scale * (smallest_normal / 256.0), small, normal)


def encode_kernel(chunk, base_hbm, inner_hbm, decoded_ref, base_ref, inner_ref, sems):
    parts = range(base_ref.shape[0] // chunk)

    def arriving(part):
        rows = pl.ds(part * chunk, chunk)
        return [
            pltpu.make_async_copy(source.at[rows], target.at[rows], sems.at[which, part])
            for which, (source, target) in enumerate(
                [(base_hbm, base_ref), (inner_hbm, inner_ref)]
            )
        ]

    for part in parts:
        for each in arriving(part):
            each.start()
    for part in parts:
        for each in arriving(part):
            each.wait()
        rows = pl.ds(part * chunk, chunk)
        for at in range(0, base_ref.shape[1], BLOCK):
            lanes = pl.ds(at, BLOCK)
            decoded = encoded(base_ref[rows, lanes], inner_ref[rows, lanes])
            decoded_ref[rows, lanes] = decoded.astype(decoded_ref.dtype)


def decoded_deltas(base_weights, replica_copy):
    rows, columns = base_weights.shape
    chunk = rows // 4
    return pl.pallas_call(
        lambda *refs: encode_kernel(chunk, *refs),
        in_specs=[pl.BlockSpec(memory_space=pltpu.HBM)] * 2,
        out_specs=pl.BlockSpec(memory_space=pltpu.VMEM),
        out_shape=jax.ShapeDtypeStruct((rows, columns), jnp.bfloat16),
        scratch_shapes=[
            pltpu.VMEM((rows, columns), jnp.float32),
            pltpu.VMEM((rows, columns), jnp.bfloat16),
            pltpu.SemaphoreType.DMA((2, 4)),
        ],
        compiler_params=pltpu.CompilerParams(vmem_limit_bytes=53 * 2**20),
        cost_estimate=pl.CostEstimate(
            flops=20 * rows * columns, bytes_accessed=8 * rows * columns, transcendentals=0
        ),
    )(base_weights, replica_copy)


def outputs_kernel(chunk, base_ref, blended_ref, steps_ref, kept_ref, grad_ref, clip_ref, *refs):
    out_refs, held_refs, sems = refs[:3], refs[3:6], refs[6]
    base_held, momentum_held, inner_held = held_refs

    def copy(which, part, rows):
        return pltpu.make_async_copy(
            held_refs[which].at[rows], out_refs[which].at[rows], sems.at[which, part]
        )

    copies = []
    momentum_held[...] = kept_ref[...] + clip_ref[...] * grad_ref[...]
    copies.append(copy(1, 0, pl.ds(0, momentum_held.shape[0])))
    copies[-1].start()
    for part in range(base_held.shape[0] // chunk):
        rows = pl.ds(part * chunk, chunk)
        steps = steps_ref[rows]
        base_held[rows] = base_ref[rows] - steps
        copies.append(copy(0, part, rows))
        copies[-1].start()
        inner_held[rows] = (blended_ref[rows] - (1.0 - blend_share) * steps).astype(jnp.bfloat16)
        copies.append(copy(2, part, rows))
        copies[-1].start()
    for each in copies:
        each.wait()


def outputs(base_weights, blended, steps, kept, outer_grad, clip_factor):
    rows, columns = base_weights.shape
    chunk = rows // 2
    shapes = (
        jax.ShapeDtypeStruct((rows, columns), jnp.float32),
        jax.ShapeDtypeStruct(kept.shape, jnp.float32),
        jax.ShapeDtypeStruct((rows, columns), jnp.bfloat16),
    )
    return pl.pallas_call(
        lambda *refs: outputs_kernel(chunk, *refs),
        in_specs=[pl.BlockSpec(memory_space=pltpu.VMEM)] * 6,
        out_specs=[pl.BlockSpec(memory_space=pl.ANY)] * 3,
        out_shape=shapes,
        scratch_shapes=[pltpu.VMEM(each.shape, each.dtype) for each in shapes]
        + [pltpu.SemaphoreType.DMA((3, 2))],
        compiler_params=pltpu.CompilerParams(vmem_limit_bytes=8 * 2**20),
        cost_estimate=pl.CostEstimate(
            flops=4 * rows * columns, bytes_accessed=18 * rows * columns, transcendentals=0
        ),
    )(base_weights, blended, steps, kept, outer_grad, clip_factor)


def lane_squares(value):
    rows, columns = value.shape
    tiles = (value * value).reshape(rows // 8, 8, columns // 128, 128)
    return tiles.sum(axis=(0, 1, 2))[None]


def lane_total(lanes, columns):
    ones = jnp.ones((lanes.shape[1], columns), lanes.dtype)
    return lax.dot(lanes, ones, precision=lax.Precision.HIGHEST)


def shards(base_weights, inner_weights, momentum):
    replicas = lax.axis_size(REPLICA)
    local_rows, columns = base_weights.shape
    owned_rows = local_rows // replicas
    decoded = decoded_deltas(base_weights, inner_weights[0])
    arrived = exchanged(decoded.reshape(replicas, owned_rows, columns), REPLICA)
    outer_grad = arrived.astype(jnp.float32).sum(axis=0) / replicas
    squares = to_everyone(lane_squares(outer_grad), RING).sum(axis=0)
    squares, base_weights, inner_weights, momentum = lax.optimization_barrier(
        (squares, base_weights, inner_weights, momentum)
    )
    replica_copy = inner_weights[0].astype(jnp.float32)
    blended = blend_share * replica_copy + (1.0 - blend_share) * base_weights
    squares, blended, kept = lax.optimization_barrier(
        (squares, blended, outer_momentum * momentum)
    )
    squares = to_everyone(squares, PLANE).sum(axis=0)
    grad_sq = lane_total(squares, columns)
    clip_factor = jnp.minimum(1.0, clip_rms / jnp.sqrt(grad_sq / (D * KVW) + epsilon))
    step_term = clip_factor * outer_grad
    step = outer_rate * (step_term + outer_momentum * (kept + step_term))
    steps = to_everyone((step * step_unit).astype(jnp.float16), REPLICA)
    steps = steps.reshape(local_rows, columns).astype(jnp.float32) * (1.0 / step_unit)
    new_base, new_momentum, new_inner = outputs(
        base_weights, blended, steps, kept, outer_grad, clip_factor
    )
    return (new_base, new_momentum, new_inner[None])


def solution(mesh):
    torus = Mesh(
        mesh.devices.reshape(4, 4, 8, 2, 2),
        ("replica_0", "replica_1", "fsdp_0", "fsdp_1", "fsdp_2"),
    )
    return jax.shard_map(
        shards,
        mesh=torus,
        in_specs=(P(FSDP, None), P(REPLICA, FSDP, None), P(FSDP_REPLICA, None)),
        out_specs=(P(FSDP, None), P(FSDP_REPLICA, None), P(REPLICA, FSDP, None)),
        check_vma=False,
    )
```

```python
import jax
import jax.numpy as jnp
from jax import lax
from jax.experimental import pallas as pl
from jax.experimental.pallas import tpu as pltpu
from jax.sharding import Mesh
from jax.sharding import PartitionSpec as P

D = 8192
KVW = 1024
BLOCK = 128
REPLICA = ("replica_0", "replica_1")
FSDP = ("fsdp_0", "fsdp_1", "fsdp_2")
FSDP_REPLICA = ("fsdp_0", "fsdp_1", "fsdp_2", "replica_0", "replica_1")
CORES = "fsdp_2"
RING = ("fsdp_1", "replica_0")
PLANE = ("replica_1", "fsdp_0")

code_limit = 448.0
outer_rate = 0.7
outer_momentum = 0.9
blend_share = 0.5
clip_rms = 0.02
epsilon = 1e-06
smallest_normal = 0.015625

step_unit = 1024.0


def exchanged(blocks, axis):
    return lax.all_to_all(blocks, axis, split_axis=0, concat_axis=0, tiled=True)


def to_everyone(value, axis):
    copies = jnp.broadcast_to(value, (lax.axis_size(axis), *value.shape))
    return exchanged(copies, axis)


def smallest_scale(peaks):
    spread = peaks * (2.0**23 + 1.0)
    near = spread - (spread - peaks)
    return jnp.where(peaks <= (code_limit / 512.0) * near, 0.5 * near, near)


def encoded(base_block, inner_block):
    deltas = base_block - inner_block.astype(jnp.float32)
    magnitude = jnp.abs(deltas)
    scale = smallest_scale(jnp.max(magnitude, axis=1, keepdims=True) + epsilon)
    beyond = deltas * (1.0 + 2.0**-23)
    spread = beyond * (2.0**20 + 1.0)
    normal = spread - (spread - beyond)
    anchor = scale * (1.5 * 2.0**6)
    small = (beyond + anchor) - anchor
    return jnp.where(magnitude < scale * (smallest_normal / 256.0), small, normal)


def encode_kernel(chunk, base_hbm, inner_hbm, decoded_ref, base_ref, inner_ref, sems):
    parts = range(base_ref.shape[0] // chunk)

    def arriving(part):
        rows = pl.ds(part * chunk, chunk)
        return [
            pltpu.make_async_copy(source.at[rows], target.at[rows], sems.at[which, part])
            for which, (source, target) in enumerate(
                [(base_hbm, base_ref), (inner_hbm, inner_ref)]
            )
        ]

    for part in parts:
        for each in arriving(part):
            each.start()
    for part in parts:
        for each in arriving(part):
            each.wait()
        rows = pl.ds(part * chunk, chunk)
        for at in range(0, base_ref.shape[1], BLOCK):
            lanes = pl.ds(at, BLOCK)
            decoded = encoded(base_ref[rows, lanes], inner_ref[rows, lanes])
            decoded_ref[rows, lanes] = decoded.astype(decoded_ref.dtype)


def decoded_deltas(base_weights, replica_copy):
    rows, columns = base_weights.shape
    chunk = rows // 4
    return pl.pallas_call(
        lambda *refs: encode_kernel(chunk, *refs),
        in_specs=[pl.BlockSpec(memory_space=pltpu.HBM)] * 2,
        out_specs=pl.BlockSpec(memory_space=pltpu.VMEM),
        out_shape=jax.ShapeDtypeStruct((rows, columns), jnp.bfloat16),
        scratch_shapes=[
            pltpu.VMEM((rows, columns), jnp.float32),
            pltpu.VMEM((rows, columns), jnp.bfloat16),
            pltpu.SemaphoreType.DMA((2, 4)),
        ],
        compiler_params=pltpu.CompilerParams(vmem_limit_bytes=53 * 2**20),
        cost_estimate=pl.CostEstimate(
            flops=20 * rows * columns, bytes_accessed=8 * rows * columns, transcendentals=0
        ),
    )(base_weights, replica_copy)


def outputs_kernel(chunk, base_ref, blended_ref, steps_ref, kept_ref, grad_ref, clip_ref, *refs):
    out_refs, held_refs, sems = refs[:3], refs[3:6], refs[6]
    base_held, momentum_held, inner_held = held_refs

    def copy(which, part, rows):
        return pltpu.make_async_copy(
            held_refs[which].at[rows], out_refs[which].at[rows], sems.at[which, part]
        )

    copies = []
    momentum_held[...] = kept_ref[...] + clip_ref[...] * grad_ref[...]
    copies.append(copy(1, 0, pl.ds(0, momentum_held.shape[0])))
    copies[-1].start()
    for part in range(base_held.shape[0] // chunk):
        rows = pl.ds(part * chunk, chunk)
        steps = steps_ref[rows]
        base_held[rows] = base_ref[rows] - steps
        copies.append(copy(0, part, rows))
        copies[-1].start()
        inner_held[rows] = (blended_ref[rows] - (1.0 - blend_share) * steps).astype(jnp.bfloat16)
        copies.append(copy(2, part, rows))
        copies[-1].start()
    for each in copies:
        each.wait()


def outputs(base_weights, blended, steps, kept, outer_grad, clip_factor):
    rows, columns = base_weights.shape
    chunk = rows // 2
    shapes = (
        jax.ShapeDtypeStruct((rows, columns), jnp.float32),
        jax.ShapeDtypeStruct(kept.shape, jnp.float32),
        jax.ShapeDtypeStruct((rows, columns), jnp.bfloat16),
    )
    return pl.pallas_call(
        lambda *refs: outputs_kernel(chunk, *refs),
        in_specs=[pl.BlockSpec(memory_space=pltpu.VMEM)] * 6,
        out_specs=[pl.BlockSpec(memory_space=pl.ANY)] * 3,
        out_shape=shapes,
        scratch_shapes=[pltpu.VMEM(each.shape, each.dtype) for each in shapes]
        + [pltpu.SemaphoreType.DMA((3, 2))],
        compiler_params=pltpu.CompilerParams(vmem_limit_bytes=8 * 2**20),
        cost_estimate=pl.CostEstimate(
            flops=4 * rows * columns, bytes_accessed=18 * rows * columns, transcendentals=0
        ),
    )(base_weights, blended, steps, kept, outer_grad, clip_factor)


def lane_squares(value):
    rows, columns = value.shape
    tiles = (value * value).reshape(rows // 8, 8, columns // 128, 128)
    return tiles.sum(axis=(0, 1, 2))[None]


def lane_total(lanes, columns):
    ones = jnp.ones((lanes.shape[1], columns), lanes.dtype)
    return lax.dot(lanes, ones, precision=lax.Precision.HIGHEST)


def shards(base_weights, inner_weights, momentum):
    replicas = lax.axis_size(REPLICA)
    local_rows, columns = base_weights.shape
    owned_rows = local_rows // replicas
    decoded = decoded_deltas(base_weights, inner_weights[0])
    arrived = exchanged(decoded.reshape(replicas, owned_rows, columns), REPLICA)
    outer_grad = arrived.astype(jnp.float32).sum(axis=0) / replicas
    squares = lax.psum(lane_squares(outer_grad), CORES)
    squares = to_everyone(squares, RING).sum(axis=0)
    squares, base_weights, inner_weights, momentum = lax.optimization_barrier(
        (squares, base_weights, inner_weights, momentum)
    )
    replica_copy = inner_weights[0].astype(jnp.float32)
    blended = blend_share * replica_copy + (1.0 - blend_share) * base_weights
    squares, blended, kept = lax.optimization_barrier(
        (squares, blended, outer_momentum * momentum)
    )
    squares = to_everyone(squares, PLANE).sum(axis=0)
    grad_sq = lane_total(squares, columns)
    clip_factor = jnp.minimum(1.0, clip_rms / jnp.sqrt(grad_sq / (D * KVW) + epsilon))
    step_term = clip_factor * outer_grad
    step = outer_rate * (step_term + outer_momentum * (kept + step_term))
    steps = to_everyone((step * step_unit).astype(jnp.float16), REPLICA)
    steps = steps.reshape(local_rows, columns).astype(jnp.float32) * (1.0 / step_unit)
    new_base, new_momentum, new_inner = outputs(
        base_weights, blended, steps, kept, outer_grad, clip_factor
    )
    return (new_base, new_momentum, new_inner[None])


def solution(mesh):
    torus = Mesh(
        mesh.devices.reshape(4, 4, 8, 2, 2),
        ("replica_0", "replica_1", "fsdp_0", "fsdp_1", "fsdp_2"),
    )
    return jax.shard_map(
        shards,
        mesh=torus,
        in_specs=(P(FSDP, None), P(REPLICA, FSDP, None), P(FSDP_REPLICA, None)),
        out_specs=(P(FSDP, None), P(FSDP_REPLICA, None), P(REPLICA, FSDP, None)),
        check_vma=False,
    )
```

```python
import jax
import jax.numpy as jnp
from jax import lax
from jax.experimental import pallas as pl
from jax.experimental.pallas import tpu as pltpu
from jax.sharding import Mesh
from jax.sharding import PartitionSpec as P

D = 8192
KVW = 1024
BLOCK = 128
REPLICA = ("replica_0", "replica_1")
FSDP = ("fsdp_0", "fsdp_1", "fsdp_2")
FSDP_REPLICA = ("fsdp_0", "fsdp_1", "fsdp_2", "replica_0", "replica_1")
RING = ("fsdp_1", "replica_0", "fsdp_2")
PLANE = ("replica_1", "fsdp_0")

code_limit = 448.0
outer_rate = 0.7
outer_momentum = 0.9
blend_share = 0.5
clip_rms = 0.02
epsilon = 1e-06
smallest_normal = 0.015625

step_unit = 1024.0


def exchanged(blocks, axis):
    return lax.all_to_all(blocks, axis, split_axis=0, concat_axis=0, tiled=True)


def to_everyone(value, axis):
    copies = jnp.broadcast_to(value, (lax.axis_size(axis), *value.shape))
    return exchanged(copies, axis)


def smallest_scale(peaks):
    spread = peaks * (2.0**23 + 1.0)
    near = spread - (spread - peaks)
    return jnp.where(peaks <= (code_limit / 512.0) * near, 0.5 * near, near)


def encoded(base_block, inner_block):
    deltas = base_block - inner_block.astype(jnp.float32)
    magnitude = jnp.abs(deltas)
    scale = smallest_scale(jnp.max(magnitude, axis=1, keepdims=True) + epsilon)
    beyond = deltas * (1.0 + 2.0**-23)
    spread = beyond * (2.0**20 + 1.0)
    normal = spread - (spread - beyond)
    anchor = scale * (1.5 * 2.0**6)
    small = (beyond + anchor) - anchor
    return jnp.where(magnitude < scale * (smallest_normal / 256.0), small, normal)


def encode_kernel(chunk, base_hbm, inner_hbm, decoded_ref, base_ref, inner_ref, sems):
    parts = range(base_ref.shape[0] // chunk)

    def arriving(part):
        rows = pl.ds(part * chunk, chunk)
        return [
            pltpu.make_async_copy(source.at[rows], target.at[rows], sems.at[which, part])
            for which, (source, target) in enumerate(
                [(base_hbm, base_ref), (inner_hbm, inner_ref)]
            )
        ]

    for part in parts:
        for each in arriving(part):
            each.start()
    for part in parts:
        for each in arriving(part):
            each.wait()
        rows = pl.ds(part * chunk, chunk)
        for at in range(0, base_ref.shape[1], BLOCK):
            lanes = pl.ds(at, BLOCK)
            decoded = encoded(base_ref[rows, lanes], inner_ref[rows, lanes])
            decoded_ref[rows, lanes] = decoded.astype(decoded_ref.dtype)


def decoded_deltas(base_weights, replica_copy):
    rows, columns = base_weights.shape
    chunk = rows // 4
    return pl.pallas_call(
        lambda *refs: encode_kernel(chunk, *refs),
        in_specs=[pl.BlockSpec(memory_space=pltpu.HBM)] * 2,
        out_specs=pl.BlockSpec(memory_space=pltpu.VMEM),
        out_shape=jax.ShapeDtypeStruct((rows, columns), jnp.bfloat16),
        scratch_shapes=[
            pltpu.VMEM((rows, columns), jnp.float32),
            pltpu.VMEM((rows, columns), jnp.bfloat16),
            pltpu.SemaphoreType.DMA((2, 4)),
        ],
        compiler_params=pltpu.CompilerParams(vmem_limit_bytes=53 * 2**20),
        cost_estimate=pl.CostEstimate(
            flops=20 * rows * columns, bytes_accessed=8 * rows * columns, transcendentals=0
        ),
    )(base_weights, replica_copy)


def outputs_kernel(chunk, base_ref, blended_ref, steps_ref, kept_ref, grad_ref, clip_ref, *refs):
    out_refs, held_refs, sems = refs[:3], refs[3:6], refs[6]
    base_held, momentum_held, inner_held = held_refs

    def copy(which, part, rows):
        return pltpu.make_async_copy(
            held_refs[which].at[rows], out_refs[which].at[rows], sems.at[which, part]
        )

    copies = []
    momentum_held[...] = kept_ref[...] + clip_ref[...] * grad_ref[...]
    copies.append(copy(1, 0, pl.ds(0, momentum_held.shape[0])))
    copies[-1].start()
    for part in range(base_held.shape[0] // chunk):
        rows = pl.ds(part * chunk, chunk)
        steps = steps_ref[rows]
        base_held[rows] = base_ref[rows] - steps
        copies.append(copy(0, part, rows))
        copies[-1].start()
        inner_held[rows] = (blended_ref[rows] - (1.0 - blend_share) * steps).astype(jnp.bfloat16)
        copies.append(copy(2, part, rows))
        copies[-1].start()
    for each in copies:
        each.wait()


def outputs(base_weights, blended, steps, kept, outer_grad, clip_factor):
    rows, columns = base_weights.shape
    chunk = rows
    shapes = (
        jax.ShapeDtypeStruct((rows, columns), jnp.float32),
        jax.ShapeDtypeStruct(kept.shape, jnp.float32),
        jax.ShapeDtypeStruct((rows, columns), jnp.bfloat16),
    )
    return pl.pallas_call(
        lambda *refs: outputs_kernel(chunk, *refs),
        in_specs=[pl.BlockSpec(memory_space=pltpu.VMEM)] * 6,
        out_specs=[pl.BlockSpec(memory_space=pl.ANY)] * 3,
        out_shape=shapes,
        scratch_shapes=[pltpu.VMEM(each.shape, each.dtype) for each in shapes]
        + [pltpu.SemaphoreType.DMA((3, 1))],
        compiler_params=pltpu.CompilerParams(vmem_limit_bytes=8 * 2**20),
        cost_estimate=pl.CostEstimate(
            flops=4 * rows * columns, bytes_accessed=18 * rows * columns, transcendentals=0
        ),
    )(base_weights, blended, steps, kept, outer_grad, clip_factor)


def lane_squares(value):
    rows, columns = value.shape
    tiles = (value * value).reshape(rows // 8, 8, columns // 128, 128)
    return tiles.sum(axis=(0, 1, 2))[None]


def lane_total(lanes, columns):
    ones = jnp.ones((lanes.shape[1], columns), lanes.dtype)
    return lax.dot(lanes, ones, precision=lax.Precision.HIGHEST)


def shards(base_weights, inner_weights, momentum):
    replicas = lax.axis_size(REPLICA)
    local_rows, columns = base_weights.shape
    owned_rows = local_rows // replicas
    decoded = decoded_deltas(base_weights, inner_weights[0])
    arrived = exchanged(decoded.reshape(replicas, owned_rows, columns), REPLICA)
    outer_grad = arrived.astype(jnp.float32).sum(axis=0) / replicas
    squares = to_everyone(lane_squares(outer_grad), RING).sum(axis=0)
    squares, base_weights, inner_weights, momentum = lax.optimization_barrier(
        (squares, base_weights, inner_weights, momentum)
    )
    replica_copy = inner_weights[0].astype(jnp.float32)
    blended = blend_share * replica_copy + (1.0 - blend_share) * base_weights
    squares, blended, kept = lax.optimization_barrier(
        (squares, blended, outer_momentum * momentum)
    )
    squares = to_everyone(squares, PLANE).sum(axis=0)
    grad_sq = lane_total(squares, columns)
    clip_factor = jnp.minimum(1.0, clip_rms / jnp.sqrt(grad_sq / (D * KVW) + epsilon))
    step_term = clip_factor * outer_grad
    step = outer_rate * (step_term + outer_momentum * (kept + step_term))
    steps = to_everyone((step * step_unit).astype(jnp.float16), REPLICA)
    steps = steps.reshape(local_rows, columns).astype(jnp.float32) * (1.0 / step_unit)
    new_base, new_momentum, new_inner = outputs(
        base_weights, blended, steps, kept, outer_grad, clip_factor
    )
    return (new_base, new_momentum, new_inner[None])


def solution(mesh):
    torus = Mesh(
        mesh.devices.reshape(4, 4, 8, 2, 2),
        ("replica_0", "replica_1", "fsdp_0", "fsdp_1", "fsdp_2"),
    )
    return jax.shard_map(
        shards,
        mesh=torus,
        in_specs=(P(FSDP, None), P(REPLICA, FSDP, None), P(FSDP_REPLICA, None)),
        out_specs=(P(FSDP, None), P(FSDP_REPLICA, None), P(REPLICA, FSDP, None)),
        check_vma=False,
    )
```

```python
import jax
import jax.numpy as jnp
from jax import lax
from jax.experimental import pallas as pl
from jax.experimental.pallas import tpu as pltpu
from jax.sharding import Mesh
from jax.sharding import PartitionSpec as P

D = 8192
KVW = 1024
BLOCK = 128
REPLICA = ("replica_0", "replica_1")
FSDP = ("fsdp_0", "fsdp_1", "fsdp_2")
FSDP_REPLICA = ("fsdp_0", "fsdp_1", "fsdp_2", "replica_0", "replica_1")
RING = ("fsdp_1", "replica_0", "fsdp_2")
PLANE = ("replica_1", "fsdp_0")

code_limit = 448.0
outer_rate = 0.7
outer_momentum = 0.9
blend_share = 0.5
clip_rms = 0.02
epsilon = 1e-06
smallest_normal = 0.015625

step_unit = 1024.0


def exchanged(blocks, axis):
    return lax.all_to_all(blocks, axis, split_axis=0, concat_axis=0, tiled=True)


def to_everyone(value, axis):
    copies = jnp.broadcast_to(value, (lax.axis_size(axis), *value.shape))
    return exchanged(copies, axis)


def smallest_scale(peaks):
    spread = peaks * (2.0**23 + 1.0)
    near = spread - (spread - peaks)
    return jnp.where(peaks <= (code_limit / 512.0) * near, 0.5 * near, near)


def encoded(base_block, inner_block):
    deltas = base_block - inner_block.astype(jnp.float32)
    magnitude = jnp.abs(deltas)
    scale = smallest_scale(jnp.max(magnitude, axis=1, keepdims=True) + epsilon)
    beyond = deltas * (1.0 + 2.0**-23)
    spread = beyond * (2.0**20 + 1.0)
    normal = spread - (spread - beyond)
    anchor = scale * (1.5 * 2.0**6)
    small = (beyond + anchor) - anchor
    return jnp.where(magnitude < scale * (smallest_normal / 256.0), small, normal)


def encode_kernel(chunk, base_hbm, inner_hbm, decoded_ref, base_ref, inner_ref, sems):
    parts = range(base_ref.shape[0] // chunk)

    def arriving(part):
        rows = pl.ds(part * chunk, chunk)
        return [
            pltpu.make_async_copy(source.at[rows], target.at[rows], sems.at[which, part])
            for which, (source, target) in enumerate(
                [(base_hbm, base_ref), (inner_hbm, inner_ref)]
            )
        ]

    for part in parts:
        for each in arriving(part):
            each.start()
    for part in parts:
        for each in arriving(part):
            each.wait()
        rows = pl.ds(part * chunk, chunk)
        for at in range(0, base_ref.shape[1], BLOCK):
            lanes = pl.ds(at, BLOCK)
            decoded = encoded(base_ref[rows, lanes], inner_ref[rows, lanes])
            decoded_ref[rows, lanes] = decoded.astype(decoded_ref.dtype)


def decoded_deltas(base_weights, replica_copy):
    rows, columns = base_weights.shape
    chunk = rows // 2
    return pl.pallas_call(
        lambda *refs: encode_kernel(chunk, *refs),
        in_specs=[pl.BlockSpec(memory_space=pltpu.HBM)] * 2,
        out_specs=pl.BlockSpec(memory_space=pltpu.VMEM),
        out_shape=jax.ShapeDtypeStruct((rows, columns), jnp.bfloat16),
        scratch_shapes=[
            pltpu.VMEM((rows, columns), jnp.float32),
            pltpu.VMEM((rows, columns), jnp.bfloat16),
            pltpu.SemaphoreType.DMA((2, 2)),
        ],
        compiler_params=pltpu.CompilerParams(vmem_limit_bytes=53 * 2**20),
        cost_estimate=pl.CostEstimate(
            flops=20 * rows * columns, bytes_accessed=8 * rows * columns, transcendentals=0
        ),
    )(base_weights, replica_copy)


def outputs_kernel(chunk, base_ref, blended_ref, steps_ref, kept_ref, grad_ref, clip_ref, *refs):
    out_refs, held_refs, sems = refs[:3], refs[3:6], refs[6]
    base_held, momentum_held, inner_held = held_refs

    def copy(which, part, rows):
        return pltpu.make_async_copy(
            held_refs[which].at[rows], out_refs[which].at[rows], sems.at[which, part]
        )

    copies = []
    momentum_held[...] = kept_ref[...] + clip_ref[...] * grad_ref[...]
    copies.append(copy(1, 0, pl.ds(0, momentum_held.shape[0])))
    copies[-1].start()
    for part in range(base_held.shape[0] // chunk):
        rows = pl.ds(part * chunk, chunk)
        steps = steps_ref[rows]
        base_held[rows] = base_ref[rows] - steps
        copies.append(copy(0, part, rows))
        copies[-1].start()
        inner_held[rows] = (blended_ref[rows] - (1.0 - blend_share) * steps).astype(jnp.bfloat16)
        copies.append(copy(2, part, rows))
        copies[-1].start()
    for each in copies:
        each.wait()


def outputs(base_weights, blended, steps, kept, outer_grad, clip_factor):
    rows, columns = base_weights.shape
    chunk = rows // 2
    shapes = (
        jax.ShapeDtypeStruct((rows, columns), jnp.float32),
        jax.ShapeDtypeStruct(kept.shape, jnp.float32),
        jax.ShapeDtypeStruct((rows, columns), jnp.bfloat16),
    )
    return pl.pallas_call(
        lambda *refs: outputs_kernel(chunk, *refs),
        in_specs=[pl.BlockSpec(memory_space=pltpu.VMEM)] * 6,
        out_specs=[pl.BlockSpec(memory_space=pl.ANY)] * 3,
        out_shape=shapes,
        scratch_shapes=[pltpu.VMEM(each.shape, each.dtype) for each in shapes]
        + [pltpu.SemaphoreType.DMA((3, 2))],
        compiler_params=pltpu.CompilerParams(vmem_limit_bytes=8 * 2**20),
        cost_estimate=pl.CostEstimate(
            flops=4 * rows * columns, bytes_accessed=18 * rows * columns, transcendentals=0
        ),
    )(base_weights, blended, steps, kept, outer_grad, clip_factor)


def lane_squares(value):
    rows, columns = value.shape
    tiles = (value * value).reshape(rows // 8, 8, columns // 128, 128)
    return tiles.sum(axis=(0, 1, 2))[None]


def lane_total(lanes, columns):
    ones = jnp.ones((lanes.shape[1], columns), lanes.dtype)
    return lax.dot(lanes, ones, precision=lax.Precision.HIGHEST)


def shards(base_weights, inner_weights, momentum):
    replicas = lax.axis_size(REPLICA)
    local_rows, columns = base_weights.shape
    owned_rows = local_rows // replicas
    decoded = decoded_deltas(base_weights, inner_weights[0])
    arrived = exchanged(decoded.reshape(replicas, owned_rows, columns), REPLICA)
    outer_grad = arrived.astype(jnp.float32).sum(axis=0) / replicas
    squares = to_everyone(lane_squares(outer_grad), RING).sum(axis=0)
    squares, base_weights, inner_weights, momentum = lax.optimization_barrier(
        (squares, base_weights, inner_weights, momentum)
    )
    replica_copy = inner_weights[0].astype(jnp.float32)
    blended = blend_share * replica_copy + (1.0 - blend_share) * base_weights
    squares, blended, kept = lax.optimization_barrier(
        (squares, blended, outer_momentum * momentum)
    )
    squares = to_everyone(squares, PLANE).sum(axis=0)
    grad_sq = lane_total(squares, columns)
    clip_factor = jnp.minimum(1.0, clip_rms / jnp.sqrt(grad_sq / (D * KVW) + epsilon))
    step_term = clip_factor * outer_grad
    step = outer_rate * (step_term + outer_momentum * (kept + step_term))
    steps = to_everyone((step * step_unit).astype(jnp.float16), REPLICA)
    steps = steps.reshape(local_rows, columns).astype(jnp.float32) * (1.0 / step_unit)
    new_base, new_momentum, new_inner = outputs(
        base_weights, blended, steps, kept, outer_grad, clip_factor
    )
    return (new_base, new_momentum, new_inner[None])


def solution(mesh):
    torus = Mesh(
        mesh.devices.reshape(4, 4, 8, 2, 2),
        ("replica_0", "replica_1", "fsdp_0", "fsdp_1", "fsdp_2"),
    )
    return jax.shard_map(
        shards,
        mesh=torus,
        in_specs=(P(FSDP, None), P(REPLICA, FSDP, None), P(FSDP_REPLICA, None)),
        out_specs=(P(FSDP, None), P(FSDP_REPLICA, None), P(REPLICA, FSDP, None)),
        check_vma=False,
    )
```
